128 devices in a mesh: dp: 16 (over x, y), rel: 8 (over z, core).
Axes of the slice: x: 4, y: 4, z: 4, core: 2. Of those that a mesh axis runs over, the one named last changes fastest.
Arguments:
- grad_out: bfloat16 [16384, 512], P('dp', 'rel'), may hold values from -6 to 6
- src_feat: bfloat16 [32768, 768], P(('dp', 'rel')), may hold values from -6 to 6
- weight: bfloat16 [768, 2560], replicated, may hold values from -0.21875 to 0.21875
- nbr_slot: int32 [16384, 64, 16], P('dp', 'rel'), may hold values from 0 to 511
- src_ids: int32 [16, 64, 512], P('dp', 'rel'), may hold values from 0 to 2047
- valid_rows: int32 [16, 64], P('dp', 'rel'), may hold values from 1 to 1024, 32768 in all within a row
- block_rel: int32 [64], P('rel'), may hold values from 0 to 4, as said below
Outputs:
- source_grad: bfloat16 [32768, 768], P(('dp', 'rel'))
- weight_grad: float32 [768, 2560], P(('dp', 'rel'))
The draws below stay inside these ranges and needn't reach their ends.
Inputs may be any that keep to these rules, and one draw needn't show every extreme that they name: `block_rel`: every one of the 5 relations owns one block or more. `valid_rows`: in each group the counts sum to 32768.
All inputs are finite; a program needn't handle non-finite values.
Results may differ from the reference program's by a relative error of at most 0.02.
Values may be sent and summed in bfloat16 or wider, within the bound.
No kernel may reach another device: no remote copies, remote signals or barrier semaphores. Data moves between devices by JAX's collectives and lax.ppermute only.
A program may use at most 128 MiB of HBM per device.

```python
import math
import jax
import jax.numpy as jnp
import numpy as np
from jax import lax

D_IN = 768
HID = 512
RELS = 5
FANOUT = 16
SRC_BLK = 512
TGT_DEV = 1024
BLK_DEV = 8
SRC_DEV = 256
GROUPS = 16
BLOCKS = 64
POOL = 2048
TARGETS = 16384
SOURCES = 32768
N_DP = 16
N_REL = 8


def draw_block_rel(key, part):
    key = jax.random.fold_in(key, 11)
    first, second, third = jax.random.split(key, 3)
    left = jax.random.randint(first, (BLOCKS,), 0, RELS)
    right = jax.random.randint(second, (BLOCKS,), 0, RELS)
    skewed = jnp.minimum(left, right)
    places = jnp.arange(BLOCKS, dtype=jnp.int32)
    base = jnp.where(places < RELS, places, skewed)
    order = jax.random.permutation(third, BLOCKS)
    return base[order].astype(jnp.int32)


def place_ends(result, stream_key, smallest, top_value):
    longest = result.shape.index(max(result.shape))
    spots = []
    for shift in (0, 1):
        where = [jax.random.randint(jax.random.fold_in(stream_key, axis), (), 0, length) for axis, length in enumerate(result.shape)]
        where[longest] = (where[longest] + shift) % result.shape[longest]
        spots.append(tuple(where))
    return result.at[spots[0]].set(smallest).at[spots[1]].set(top_value)


def block_scale(key, extent, cuts, smallest, top_value):
    level, own = 1.0, jax.random.fold_in(key, 6)
    for position, blocks in cuts:
        steps = jnp.exp(jax.random.uniform(jax.random.fold_in(own, position), (blocks,), jnp.float32, smallest / len(cuts), top_value / len(cuts)))
        level = level * jnp.repeat(steps, extent[position] // blocks).reshape([-1 if axis == position else 1 for axis in range(len(extent))])
    return level


def profile(amount, total, reach, slope):
    loads = [(1 << 20) // math.isqrt(grade ** slope) + 1 for grade in range(2, amount + 1)]
    spare, holding = total - reach - (amount - 1), [1] * (amount - 1)
    while spare > 0:
        free = [i for i in range(amount - 1) if holding[i] < reach]
        whole, left = sum([loads[i] for i in free]), spare
        for i in free:
            addition = min(reach - holding[i], max(1, left * loads[i] // whole), spare)
            holding[i] = holding[i] + addition
            spare = spare - addition
    return np.array([reach] + holding)


def uneven_parts(rng, count, total, bound, skew):
    if count == 2:
        one = jax.random.randint(rng, (), max(1, total - bound), min(bound, total - 1) + 1)
        return jnp.stack([one, total - one])
    tallies = jnp.asarray(profile(count, total, bound, skew), jnp.int32)
    twos = (count - 1) // 2
    source_of, sink = tallies[1:1 + 2 * twos:2], tallies[2:2 + 2 * twos:2]
    slack = jnp.minimum(source_of - 1, bound - sink)
    passed = jax.random.randint(jax.random.fold_in(rng, 1), (twos,), 0, 1 << 20) % (slack + 1)
    tallies = tallies.at[1:1 + 2 * twos:2].set(source_of - passed).at[2:2 + 2 * twos:2].set(sink + passed)
    return tallies[jax.random.permutation(jax.random.fold_in(rng, 2), count)]


def bell_draw(rng, dims, width, most, cuts=(), held_as=jnp.bfloat16):
    result = jax.random.normal(rng, dims, jnp.float32) * width
    if len(cuts) > 0:
        result = block_scale(rng, dims, cuts, -0.22, 0.18) * result
    return jnp.clip(result, min=-most, max=most).astype(held_as)


def setup_inputs(seed: int = 0) -> dict:
    arg_keys = jax.random.split(jax.random.key(seed), 8)
    return {
        "grad_out": bell_draw(arg_keys[0], (TARGETS, HID), 1.0, 6.0, ((0, 16), (1, 8))),
        "src_feat": bell_draw(arg_keys[1], (SOURCES, D_IN), 1.0, 6.0, ((0, 128),)),
        "weight": bell_draw(arg_keys[2], (D_IN, RELS * HID), D_IN ** -0.5, 0.21875),
        "nbr_slot": place_ends(jax.random.randint(arg_keys[3], (TARGETS, BLOCKS, FANOUT), 0, SRC_BLK), jax.random.fold_in(arg_keys[3], 1), 0, SRC_BLK - 1).astype(jnp.int32),
        "src_ids": place_ends(jax.random.randint(arg_keys[4], (GROUPS, BLOCKS, SRC_BLK), 0, POOL), jax.random.fold_in(arg_keys[4], 1), 0, POOL - 1).astype(jnp.int32),
        "valid_rows": jax.vmap(lambda own: uneven_parts(own, BLOCKS, BLOCKS * TGT_DEV // 2, TGT_DEV, 2))(jax.random.split(arg_keys[5], GROUPS)).reshape((GROUPS, BLOCKS)).astype(jnp.int32),
        "block_rel": draw_block_rel(jax.random.fold_in(arg_keys[7], 71), 0),
    }


def reference(grad_out, src_feat, weight, nbr_slot, src_ids, valid_rows, block_rel):
    blocks = BLK_DEV * N_REL
    pool_size = SRC_DEV * N_REL
    weight3 = weight.astype(jnp.float32).reshape(D_IN, RELS, HID)
    positions = jnp.arange(TGT_DEV, dtype=jnp.int32)

    def one_group(total, group):
        start = (group * TGT_DEV).astype(jnp.int32)
        grads = lax.dynamic_slice_in_dim(grad_out, start, TGT_DEV, 0).astype(jnp.float32)
        feats = lax.dynamic_slice_in_dim(src_feat, (group * pool_size).astype(jnp.int32), pool_size, 0)
        slots = lax.dynamic_slice_in_dim(nbr_slot, start, TGT_DEV, 0)
        ids = src_ids[group]
        valid = valid_rows[group]
        back = jnp.einsum("th,drh->rtd", grads, weight3).astype(jnp.bfloat16).astype(jnp.float32)

        def one_block(carry, b):
            sums, parts = carry
            nodes = ids[b][slots[:, b, :]]
            share = (positions < valid[b]).astype(jnp.float32) / FANOUT
            rows = jnp.take(feats, nodes, axis=0).astype(jnp.float32)
            message = jnp.sum(rows, axis=1) * share[:, None]
            sums = sums.at[block_rel[b]].add(message)
            values = back[block_rel[b]] * share[:, None]
            spread = jnp.broadcast_to(values[:, None, :], (TGT_DEV, FANOUT, D_IN))
            parts = parts.at[b // BLK_DEV, nodes].add(spread)
            return (sums, parts), None

        init = (jnp.zeros((RELS, TGT_DEV, D_IN), jnp.float32), jnp.zeros((N_REL, pool_size, D_IN), jnp.float32))
        (sums, parts), _ = lax.scan(one_block, init, jnp.arange(blocks, dtype=jnp.int32))
        agg = sums.astype(jnp.bfloat16).astype(jnp.float32)
        rounded = lax.optimization_barrier(parts.astype(jnp.bfloat16))
        source_part = jnp.sum(rounded.astype(jnp.float32), axis=0).astype(jnp.bfloat16)
        total = total + jnp.einsum("rtd,th->drh", agg, grads)
        return total, source_part

    total, pieces = lax.scan(one_group, jnp.zeros((D_IN, RELS, HID), jnp.float32), jnp.arange(N_DP, dtype=jnp.int32))
    source_grad = pieces.reshape(N_DP * pool_size, D_IN)
    weight_grad = (total * (TARGETS ** -0.5)).reshape(D_IN, RELS * HID)
    return source_grad, weight_grad
```

```python
import jax
import jax.numpy as jnp
from jax import lax
from jax.experimental import pallas as pl
from jax.experimental.pallas import tpu as pltpu
from jax.sharding import PartitionSpec as P

I32 = jnp.int32
BF16 = jnp.bfloat16
F32 = jnp.float32
D_IN = 768
HID = 512
RELS = 5
COLS = RELS * HID
FANOUT = 16
SLOTS = 512
TGT = 1024
BLKS = 8
POOL = 2048
OWN = 256
NO_EDGE = RELS * POOL
TILE = 256
PLANES = 10
SLICE = COLS // 8
ROWS_OUT = 6
LANES = 128


def edge_kernel(valid_ref, rel_ref, ids_ref, nbr_ref, out_ref):
    lane = lax.broadcasted_iota(I32, (8, LANES), 1)
    sub = lax.broadcasted_iota(I32, (8, LANES), 0)
    meta = jnp.zeros((8, LANES), I32)
    for b in range(BLKS):
        rel = rel_ref[b]
        limit = valid_ref[0, b]
        meta = jnp.where((sub == b) & (lane == 0), rel, meta)
        meta = jnp.where((sub == b) & (lane == 1), (limit + (TILE - 1)) // TILE, meta)
        node = ids_ref[b : b + 1, :]
        code = rel * POOL + (node & 1792) + ((node & 7) << 5) + ((node >> 3) & 31)
        tables = [
            jnp.broadcast_to(code[:, i * LANES : (i + 1) * LANES], (8, LANES))
            for i in range(SLOTS // LANES)
        ]
        for t in range(TGT // LANES):
            cols = slice(t * LANES, (t + 1) * LANES)
            live = (lane + t * LANES) < limit
            halves = []
            for half in range(2):
                slot = nbr_ref[b, half * 8 : (half + 1) * 8, cols]
                low = slot & (LANES - 1)
                high = slot >> 7
                got = [
                    jnp.take_along_axis(table, low, axis=1, mode="promise_in_bounds")
                    for table in tables
                ]
                found = jnp.where(
                    high < 2,
                    jnp.where(high == 0, got[0], got[1]),
                    jnp.where(high == 2, got[2], got[3]),
                )
                halves.append(jnp.where(live, found, NO_EDGE))
            out_ref[b, :, cols] = halves[0] | (halves[1] << 16)
    out_ref[BLKS, :, 0:LANES] = meta
    out_ref[BLKS, :, LANES:TGT] = jnp.zeros((8, TGT - LANES), I32)


def edge_codes(valid_rows, block_rel, ids, nbr):
    return pl.pallas_call(
        edge_kernel,
        out_shape=jax.ShapeDtypeStruct((BLKS + 1, 8, TGT), I32),
        in_specs=[pl.BlockSpec(memory_space=pltpu.SMEM)] * 2
        + [pl.BlockSpec(memory_space=pltpu.VMEM)] * 2,
        out_specs=pl.BlockSpec(memory_space=pltpu.VMEM),
        cost_estimate=pl.CostEstimate(flops=0, bytes_accessed=1 << 20, transcendentals=0),
        name="edge_codes",
    )(valid_rows, block_rel, ids, nbr)


def full_add(a, b, c):
    x = a ^ b
    return x ^ c, (a & b) | (c & x)


def count_bits(masks, planes):
    carried = masks
    out = []
    for i in range(PLANES):
        cur = carried + [planes[i]]
        carried = []
        while len(cur) >= 3:
            s, c = full_add(cur[0], cur[1], cur[2])
            cur = cur[3:] + [s]
            carried.append(c)
        if len(cur) == 2:
            carried.append(cur[0] & cur[1])
            cur = [cur[0] ^ cur[1]]
        out.append(cur[0])
    return out


def swap_bits(a, b, shift, mask):
    t = (lax.shift_right_logical(a, jnp.int32(shift)) ^ b) & mask
    return a ^ (t << shift), b ^ t


def plane_bytes(planes):
    x = list(planes)
    for shift, mask in ((4, 0x0F0F0F0F), (2, 0x33333333), (1, 0x55555555)):
        for i in range(8):
            if not i & shift:
                x[i], x[i + shift] = swap_bits(x[i], x[i + shift], shift, mask)
    return x


def counts(planes):
    low = plane_bytes(planes[:8])
    rows = [None] * 32
    for off in range(8):
        high = None
        for i in range(8, PLANES):
            f = lax.shift_right_logical(planes[i], jnp.int32(off)) & 0x01010101
            f = f << (i - 8)
            high = f if high is None else high | f
        for q in range(4):
            a = lax.shift_right_logical(low[off], jnp.int32(8 * q)) & 255
            h = lax.shift_right_logical(high, jnp.int32(8 * q)) & 3
            rows[off + 8 * q] = (a | (h << 8)).astype(F32)
    return jnp.concatenate(rows, axis=0).astype(BF16)


def hidden_kernel(place_ref, *refs):
    edges = refs[:8]
    grads_ref, weight_ref = refs[8:10]
    source_ref = refs[10]
    pieces = refs[11:19]
    planes_ref, keys, meta, weight_vmem, adj, hidden, meta_sems, weight_sem = refs[19:]
    mine, x, core = place_ref[0], place_ref[1], place_ref[2]
    fetch = pltpu.make_async_copy(weight_ref, weight_vmem, weight_sem)
    fetch.start()
    metas = [
        pltpu.make_async_copy(edges[i].at[BLKS, :, pl.ds(0, LANES)], meta.at[i], meta_sems.at[i])
        for i in range(8)
    ]
    for copy in metas:
        copy.start()
    planes_ref[...] = jnp.zeros_like(planes_ref)
    row = lax.broadcasted_iota(I32, (8, TILE), 0)
    for copy in metas:
        copy.wait()
    for i in range(8):

        def one_block(b, carry, i=i):
            rel = meta[i, b, 0]
            tiles = meta[i, b, 1]
            word = edges[i][b]
            for half, code in enumerate((word & 0xFFFF, word >> 16)):
                keys[half, 0] = code >> 5
                keys[half, 1] = jnp.left_shift(jnp.int32(1), code & 31)
            target = row + (rel * (POOL // 32) + mine * (OWN // 32))

            def one_tile(t, carry):
                cols = pl.ds(pl.multiple_of(t * TILE, TILE), TILE)
                masks = []
                for half in range(2):
                    for s in range(8):
                        key = jnp.broadcast_to(keys[half, 0, pl.ds(s, 1), cols], (8, TILE))
                        bit = jnp.broadcast_to(keys[half, 1, pl.ds(s, 1), cols], (8, TILE))
                        masks.append(jnp.where(key == target, bit, 0))
                new = count_bits(masks, [planes_ref[rel, p, :, cols] for p in range(PLANES)])
                for p in range(PLANES):
                    planes_ref[rel, p, :, cols] = new[p]
                return carry

            return lax.fori_loop(0, tiles, one_tile, carry)

        lax.fori_loop(0, BLKS, one_block, 0)
    fetch.wait()
    total = None
    for r in range(RELS):

        def one_part(t, carry, r=r):
            cols = pl.ds(pl.multiple_of(t * LANES, LANES), LANES)
            adj[:, cols] = counts([planes_ref[r, p, :, cols] for p in range(PLANES)])
            return carry

        lax.fori_loop(0, TGT // LANES, one_part, 0)
        h = lax.dot_general(
            adj[...], grads_ref[...], (((1,), (1,)), ((), ())), preferred_element_type=F32
        )
        h = (h * (1.0 / FANOUT)).astype(BF16)
        term = lax.dot_general(
            h,
            weight_vmem[:, r * HID : (r + 1) * HID],
            (((1,), (1,)), ((), ())),
            preferred_element_type=F32,
        )
        total = term if total is None else total + term
        ht = h.T
        for q in range(HID // 64):
            at = r * (HID // 64) + q
            s, within = at // 5, at % 5
            pos = (s // 4 ^ core) * 4 + ((s % 4 - x) & 3)
            start = pl.multiple_of(pos * SLICE + within * 64, 64)
            hidden[pl.ds(start, 64), :] = ht[q * 64 : (q + 1) * 64, :]
    source_ref[...] = total.astype(BF16)
    for i in range(8):
        pieces[i][...] = hidden[i * SLICE : (i + 1) * SLICE, :]


def hidden_parts(place, edges, grads, weight):
    vmem = pl.BlockSpec(memory_space=pltpu.VMEM)
    return pl.pallas_call(
        hidden_kernel,
        out_shape=[jax.ShapeDtypeStruct((OWN, D_IN), BF16)]
        + [jax.ShapeDtypeStruct((SLICE, OWN), BF16)] * 8,
        in_specs=[pl.BlockSpec(memory_space=pltpu.SMEM)]
        + [vmem] * 9
        + [pl.BlockSpec(memory_space=pl.ANY)],
        out_specs=[vmem] * 9,
        scratch_shapes=[
            pltpu.VMEM((RELS, PLANES, 8, TGT), I32),
            pltpu.VMEM((2, 2, 8, TGT), I32),
            pltpu.SMEM((8, 8, LANES), I32),
            pltpu.VMEM((D_IN, COLS), BF16),
            pltpu.VMEM((OWN, TGT), BF16),
            pltpu.VMEM((COLS, OWN), BF16),
            pltpu.SemaphoreType.DMA((8,)),
            pltpu.SemaphoreType.DMA,
        ],
        compiler_params=pltpu.CompilerParams(vmem_limit_bytes=40 << 20),
        cost_estimate=pl.CostEstimate(
            flops=14_000_000_000, bytes_accessed=9 << 20, transcendentals=0
        ),
        name="hidden_parts",
    )(place, *edges, grads, weight)


def product_kernel(*refs):
    hiddens, pools = refs[:8], refs[8:16]
    out_ref, flat, chunks = refs[16:]
    total = None
    for i in range(8):
        term = jnp.dot(hiddens[i][...], pools[i][...], preferred_element_type=F32)
        total = term if total is None else total + term
    for r in range(ROWS_OUT):
        flat[:, r * SLICE : (r + 1) * SLICE] = total[:, r * LANES : (r + 1) * LANES].T
    for c in range(15):
        chunks[:, c, :] = flat[:, c * LANES : (c + 1) * LANES]
    chunks[:, 15, :] = jnp.zeros((LANES, LANES), F32)
    out_ref[...] = chunks[...].astype(BF16)


def products(hiddens, pools):
    vmem = pl.BlockSpec(memory_space=pltpu.VMEM)
    return pl.pallas_call(
        product_kernel,
        out_shape=jax.ShapeDtypeStruct((LANES, 16, LANES), BF16),
        in_specs=[vmem] * 16,
        out_specs=vmem,
        scratch_shapes=[
            pltpu.VMEM((LANES, ROWS_OUT * SLICE), F32),
            pltpu.VMEM((LANES, 16, LANES), F32),
        ],
        compiler_params=pltpu.CompilerParams(vmem_limit_bytes=40 << 20),
        cost_estimate=pl.CostEstimate(
            flops=1_000_000_000, bytes_accessed=5 << 20, transcendentals=0
        ),
        name="products",
    )(*hiddens, *pools)


def on_device(grad_out, src_feat, weight, nbr_slot, src_ids, valid_rows, block_rel):
    dp, rel = lax.axis_index("dp"), lax.axis_index("rel")
    place = jnp.stack([rel, dp // 4, rel % 2]).astype(I32)

    def along_z(v, k):
        return lax.ppermute(v, "rel", [(i, (i + 2 * k) % 8) for i in range(8)])

    def other_core(v):
        return lax.ppermute(v, "rel", [(i, i ^ 1) for i in range(8)])

    def along_x(v, k):
        return lax.ppermute(v, "dp", [(i, (i + 4 * k) % 16) for i in range(16)])

    grads = lax.all_gather(grad_out.T, "rel", axis=0, tiled=True)
    codes = edge_codes(valid_rows, block_rel, src_ids[0], nbr_slot.transpose(1, 2, 0))
    mine = [codes] + [along_z(codes, k) for k in (1, 2, 3)]
    edges = mine + [other_core(v) for v in mine]

    old = jnp.arange(D_IN, dtype=I32)[:, None]
    new = jnp.arange(D_IN, dtype=I32)[None, :]
    order = (old == (new % LANES) * ROWS_OUT + new // LANES).astype(BF16)
    feats = jnp.dot(src_feat, order, preferred_element_type=F32).astype(BF16)
    near = [feats] + [along_x(feats, k) for k in (1, 2, 3)]
    pools = near + [other_core(v) for v in near]

    source_grad, *parts = hidden_parts(place, edges, grads, weight)
    own = parts[:4]
    far = [other_core(v) for v in parts[4:]]
    hiddens = [own[0]] + [along_x(own[k], k) for k in (1, 2, 3)]
    hiddens += [far[0]] + [along_x(far[k], k) for k in (1, 2, 3)]
    chunks = products(hiddens, pools)
    got = lax.all_to_all(chunks, ("dp", "rel"), 0, 0, tiled=True)
    got = got.reshape(4, 16, 2, 16 * LANES).astype(F32)
    summed = jnp.sum(got, axis=1)[:, :, : ROWS_OUT * SLICE]
    summed = summed.reshape(4, 2, ROWS_OUT, SLICE).transpose(2, 1, 0, 3).reshape(ROWS_OUT, COLS)
    scale = float(TGT * 16) ** (-0.5)
    return source_grad, summed * scale


def solution(mesh):
    return jax.shard_map(
        on_device,
        mesh=mesh,
        in_specs=(
            P("dp", "rel"),
            P(("dp", "rel"), None),
            P(),
            P("dp", "rel", None),
            P("dp", "rel", None),
            P("dp", "rel"),
            P("rel"),
        ),
        out_specs=(P(("dp", "rel"), None), P(("dp", "rel"), None)),
        check_vma=False,
    )
```

```python
import functools

import jax
import jax.numpy as jnp
from jax import lax
from jax.experimental import pallas as pl
from jax.experimental.pallas import tpu as pltpu
from jax.sharding import PartitionSpec as P

I32 = jnp.int32
BF16 = jnp.bfloat16
F32 = jnp.float32
D_IN = 768
HID = 512
RELS = 5
COLS = RELS * HID
FANOUT = 16
SLOTS = 512
TGT = 1024
BLKS = 8
POOL = 2048
OWN = 256
NO_EDGE = RELS * POOL
TILE = 256
PLANES = 10
HALF = COLS // 2
ROWS_OUT = 6
LANES = 128
CHUNK = 64
DEVICES = 128


def edge_kernel(valid_ref, rel_ref, ids_ref, nbr_ref, out_ref):
    lane = lax.broadcasted_iota(I32, (8, LANES), 1)
    sub = lax.broadcasted_iota(I32, (8, LANES), 0)
    meta = jnp.zeros((8, LANES), I32)
    for b in range(BLKS):
        rel = rel_ref[b]
        limit = valid_ref[0, b]
        meta = jnp.where((sub == b) & (lane == 0), rel, meta)
        meta = jnp.where((sub == b) & (lane == 1), (limit + (TILE - 1)) // TILE, meta)
        node = ids_ref[b : b + 1, :]
        code = rel * POOL + (node & 1792) + ((node & 7) << 5) + ((node >> 3) & 31)
        tables = [
            jnp.broadcast_to(code[:, i * LANES : (i + 1) * LANES], (8, LANES))
            for i in range(SLOTS // LANES)
        ]
        for t in range(TGT // LANES):
            cols = slice(t * LANES, (t + 1) * LANES)
            live = (lane + t * LANES) < limit
            halves = []
            for half in range(2):
                slot = nbr_ref[b, half * 8 : (half + 1) * 8, cols]
                low = slot & (LANES - 1)
                high = slot >> 7
                got = [
                    jnp.take_along_axis(table, low, axis=1, mode="promise_in_bounds")
                    for table in tables
                ]
                found = jnp.where(
                    high < 2,
                    jnp.where(high == 0, got[0], got[1]),
                    jnp.where(high == 2, got[2], got[3]),
                )
                halves.append(jnp.where(live, found, NO_EDGE))
            out_ref[b, :, cols] = halves[0] | (halves[1] << 16)
    out_ref[BLKS, :, 0:LANES] = meta
    out_ref[BLKS, :, LANES:TGT] = jnp.zeros((8, TGT - LANES), I32)


def edge_codes(valid_rows, block_rel, ids, nbr):
    return pl.pallas_call(
        edge_kernel,
        out_shape=jax.ShapeDtypeStruct((BLKS + 1, 8, TGT), I32),
        in_specs=[pl.BlockSpec(memory_space=pltpu.SMEM)] * 2
        + [pl.BlockSpec(memory_space=pltpu.VMEM)] * 2,
        out_specs=pl.BlockSpec(memory_space=pltpu.VMEM),
        cost_estimate=pl.CostEstimate(flops=0, bytes_accessed=1 << 20, transcendentals=0),
        name="edge_codes",
    )(valid_rows, block_rel, ids, nbr)


def full_add(a, b, c):
    x = a ^ b
    return x ^ c, (a & b) | (c & x)


def count_bits(masks, planes):
    carried = masks
    out = []
    for i in range(PLANES):
        cur = carried + [planes[i]]
        carried = []
        while len(cur) >= 3:
            s, c = full_add(cur[0], cur[1], cur[2])
            cur = cur[3:] + [s]
            carried.append(c)
        if len(cur) == 2:
            carried.append(cur[0] & cur[1])
            cur = [cur[0] ^ cur[1]]
        out.append(cur[0])
    return out


def swap_bits(a, b, shift, mask):
    t = (lax.shift_right_logical(a, jnp.int32(shift)) ^ b) & mask
    return a ^ (t << shift), b ^ t


def plane_bytes(planes):
    x = list(planes)
    for shift, mask in ((4, 0x0F0F0F0F), (2, 0x33333333), (1, 0x55555555)):
        for i in range(8):
            if not i & shift:
                x[i], x[i + shift] = swap_bits(x[i], x[i + shift], shift, mask)
    return x


def counts(planes):
    low = plane_bytes(planes[:8])
    rows = [None] * 32
    for off in range(8):
        high = None
        for i in range(8, PLANES):
            f = lax.shift_right_logical(planes[i], jnp.int32(off)) & 0x01010101
            f = f << (i - 8)
            high = f if high is None else high | f
        for q in range(4):
            a = lax.shift_right_logical(low[off], jnp.int32(8 * q)) & 255
            h = lax.shift_right_logical(high, jnp.int32(8 * q)) & 3
            rows[off + 8 * q] = (a | (h << 8)).astype(F32)
    return jnp.concatenate(rows, axis=0).astype(BF16)


def count_kernel(n, first, place_ref, *refs):
    edges = refs[:n]
    at = n if first else n + 1
    planes_ref, words, keys, meta, meta_sems, word_sems = refs[at:]
    if first:
        planes_ref[...] = jnp.zeros_like(planes_ref)
    else:
        planes_ref[...] = refs[n][...]
    mine = place_ref[0]
    metas = [
        pltpu.make_async_copy(edges[i].at[BLKS, :, pl.ds(0, LANES)], meta.at[i], meta_sems.at[i])
        for i in range(n)
    ]
    loads = [
        pltpu.make_async_copy(edges[i].at[pl.ds(0, BLKS)], words.at[i], word_sems.at[i])
        for i in range(n)
    ]
    for m, w in zip(metas, loads):
        m.start()
        w.start()
    row = lax.broadcasted_iota(I32, (8, TILE), 0)
    for i in range(n):
        metas[i].wait()
        loads[i].wait()

        def one_block(b, carry, i=i):
            rel = meta[i, b, 0]
            tiles = meta[i, b, 1]
            word = words[i, b]
            for half, code in enumerate((word & 0xFFFF, word >> 16)):
                keys[half, 0] = code >> 5
                keys[half, 1] = jnp.left_shift(jnp.int32(1), code & 31)
            target = row + (rel * (POOL // 32) + mine * (OWN // 32))

            def one_tile(t, carry):
                cols = pl.ds(pl.multiple_of(t * TILE, TILE), TILE)
                masks = []
                for half in range(2):
                    for s in range(8):
                        key = jnp.broadcast_to(keys[half, 0, pl.ds(s, 1), cols], (8, TILE))
                        bit = jnp.broadcast_to(keys[half, 1, pl.ds(s, 1), cols], (8, TILE))
                        masks.append(jnp.where(key == target, bit, 0))
                new = count_bits(masks, [planes_ref[rel, p, :, cols] for p in range(PLANES)])
                for p in range(PLANES):
                    planes_ref[rel, p, :, cols] = new[p]
                return carry

            return lax.fori_loop(0, tiles, one_tile, carry)

        lax.fori_loop(0, BLKS, one_block, 0)


def count_edges(place, edges, planes=None):
    n = len(edges)
    vmem = pl.BlockSpec(memory_space=pltpu.VMEM)
    anywhere = pl.BlockSpec(memory_space=pl.ANY)
    first = planes is None
    return pl.pallas_call(
        functools.partial(count_kernel, n, first),
        out_shape=jax.ShapeDtypeStruct((RELS, PLANES, 8, TGT), I32),
        in_specs=[pl.BlockSpec(memory_space=pltpu.SMEM)]
        + [anywhere] * n
        + ([] if first else [vmem]),
        out_specs=vmem,
        scratch_shapes=[
            pltpu.VMEM((n, BLKS, 8, TGT), I32),
            pltpu.VMEM((2, 2, 8, TGT), I32),
            pltpu.SMEM((n, 8, LANES), I32),
            pltpu.SemaphoreType.DMA((n,)),
            pltpu.SemaphoreType.DMA((n,)),
        ],
        compiler_params=pltpu.CompilerParams(vmem_limit_bytes=14 << 20),
        cost_estimate=pl.CostEstimate(
            flops=n * 1_000_000_000, bytes_accessed=n << 19, transcendentals=0
        ),
        name="count_edges",
    )(place, *edges, *([] if first else [planes]))


def hidden_kernel(place_ref, planes_ref, grads_ref, own_ref, other_ref, adj):
    core = place_ref[1]
    half = HID // 2
    for r in range(RELS):

        def one_part(t, carry, r=r):
            cols = pl.ds(pl.multiple_of(t * LANES, LANES), LANES)
            adj[:, cols] = counts([planes_ref[r, p, :, cols] for p in range(PLANES)])
            return carry

        lax.fori_loop(0, TGT // LANES, one_part, 0)
        for out_ref, which in ((other_ref, 1 - core), (own_ref, core)):
            rows = pl.ds(pl.multiple_of(which * half, half), half)
            h = lax.dot_general(
                adj[...], grads_ref[rows, :], (((1,), (1,)), ((), ())), preferred_element_type=F32
            )
            out_ref[:, r * half : (r + 1) * half] = (h * (1.0 / FANOUT)).astype(BF16)


def hidden_halves(place, planes, grads):
    vmem = pl.BlockSpec(memory_space=pltpu.VMEM)
    return pl.pallas_call(
        hidden_kernel,
        out_shape=[jax.ShapeDtypeStruct((OWN, HALF), BF16)] * 2,
        in_specs=[pl.BlockSpec(memory_space=pltpu.SMEM), vmem, vmem],
        out_specs=[vmem] * 2,
        scratch_shapes=[pltpu.VMEM((OWN, TGT), BF16)],
        compiler_params=pltpu.CompilerParams(vmem_limit_bytes=16 << 20),
        cost_estimate=pl.CostEstimate(
            flops=4_000_000_000, bytes_accessed=4 << 20, transcendentals=0
        ),
        name="hidden_halves",
    )(place, planes, grads)


def source_kernel(place_ref, own_ref, other_ref, weight_ref, out_ref):
    core = place_ref[1]
    half = HID // 2
    total = None
    for r in range(RELS):
        for h_ref, which in ((own_ref, core), (other_ref, 1 - core)):
            cols = pl.ds(pl.multiple_of(r * HID + which * half, half), half)
            term = lax.dot_general(
                h_ref[:, r * half : (r + 1) * half],
                weight_ref[:, cols],
                (((1,), (1,)), ((), ())),
                preferred_element_type=F32,
            )
            total = term if total is None else total + term
    out_ref[...] = total.astype(BF16)


def source_rows(place, own, other, weight):
    vmem = pl.BlockSpec(memory_space=pltpu.VMEM)
    return pl.pallas_call(
        source_kernel,
        out_shape=jax.ShapeDtypeStruct((OWN, D_IN), BF16),
        in_specs=[pl.BlockSpec(memory_space=pltpu.SMEM)] + [vmem] * 3,
        out_specs=vmem,
        compiler_params=pltpu.CompilerParams(vmem_limit_bytes=16 << 20),
        cost_estimate=pl.CostEstimate(
            flops=1_000_000_000, bytes_accessed=6 << 20, transcendentals=0
        ),
        name="source_rows",
    )(place, own, other, weight)


def product_kernel(h0_ref, h1_ref, f0_ref, f1_ref, out_ref, chunks):
    tiles = HALF // LANES
    chunks[:, ROWS_OUT * tiles :, :] = jnp.zeros((DEVICES, CHUNK - ROWS_OUT * tiles, LANES), F32)
    for r in range(ROWS_OUT):
        rows = slice(r * LANES, (r + 1) * LANES)
        p = jnp.dot(f0_ref[rows, :], h0_ref[...], preferred_element_type=F32)
        p += jnp.dot(f1_ref[rows, :], h1_ref[...], preferred_element_type=F32)
        for c in range(tiles):
            chunks[:, r * tiles + c, :] = p[:, c * LANES : (c + 1) * LANES]
    out_ref[...] = chunks[...].astype(BF16)


def products(h0, h1, f0, f1):
    vmem = pl.BlockSpec(memory_space=pltpu.VMEM)
    return pl.pallas_call(
        product_kernel,
        out_shape=jax.ShapeDtypeStruct((DEVICES, CHUNK, LANES), BF16),
        in_specs=[vmem] * 4,
        out_specs=vmem,
        scratch_shapes=[pltpu.VMEM((DEVICES, CHUNK, LANES), F32)],
        compiler_params=pltpu.CompilerParams(vmem_limit_bytes=24 << 20),
        cost_estimate=pl.CostEstimate(
            flops=1_000_000_000, bytes_accessed=5 << 20, transcendentals=0
        ),
        name="products",
    )(h0, h1, f0, f1)


def sum_kernel(scale, got_ref, out_ref, sums):
    tiles = HALF // LANES
    totals = [None, None]
    for d in range(DEVICES):
        term = got_ref[d].astype(F32)
        core = d % 2
        totals[core] = term if totals[core] is None else totals[core] + term
    for core in range(2):
        sums[core] = totals[core] * scale
    for r in range(ROWS_OUT):
        for rel in range(RELS):
            for core in range(2):
                for part in range(2):
                    to = (rel * 4 + core * 2 + part) * LANES
                    at = r * tiles + rel * 2 + part
                    out_ref[r : r + 1, to : to + LANES] = sums[core, at : at + 1, :]


def sum_chunks(got, scale):
    vmem = pl.BlockSpec(memory_space=pltpu.VMEM)
    return pl.pallas_call(
        functools.partial(sum_kernel, scale),
        out_shape=jax.ShapeDtypeStruct((ROWS_OUT, COLS), F32),
        in_specs=[vmem],
        out_specs=vmem,
        scratch_shapes=[pltpu.VMEM((2, CHUNK, LANES), F32)],
        compiler_params=pltpu.CompilerParams(vmem_limit_bytes=14 << 20),
        cost_estimate=pl.CostEstimate(flops=1 << 20, bytes_accessed=2 << 20, transcendentals=0),
        name="sum_chunks",
    )(got)


def on_device(grad_out, src_feat, weight, nbr_slot, src_ids, valid_rows, block_rel):
    rel = lax.axis_index("rel")
    place = jnp.stack([rel, rel & 1]).astype(I32)

    def along_z(v, k):
        return lax.ppermute(v, "rel", [(i, (i + 2 * k) % 8) for i in range(8)])

    def other_core(v):
        return lax.ppermute(v, "rel", [(i, i ^ 1) for i in range(8)])

    grads = lax.all_gather(grad_out.T, "rel", axis=0, tiled=True)
    codes = edge_codes(valid_rows, block_rel, src_ids[0], nbr_slot.transpose(1, 2, 0))
    far = [along_z(codes, k) for k in (2, 1, 3)]
    near = [codes] + far
    planes = count_edges(place, near)
    planes = count_edges(place, [other_core(v) for v in near], planes)

    old = jnp.arange(D_IN, dtype=I32)[:, None]
    new = jnp.arange(D_IN, dtype=I32)[None, :]
    order = (old == (new % LANES) * ROWS_OUT + new // LANES).astype(BF16)
    feats = lax.dot_general(
        order, src_feat, (((0,), (1,)), ((), ())), preferred_element_type=F32
    ).astype(BF16)
    feats_other = other_core(feats)

    own, other = hidden_halves(place, planes, grads)
    got = other_core(other)
    source_grad = source_rows(place, own, other, weight)
    chunks = products(own, got, feats, feats_other)
    chunks = lax.all_to_all(chunks, ("dp", "rel"), 0, 0, tiled=True)
    return source_grad, sum_chunks(chunks, float(TGT * 16) ** (-0.5))


def solution(mesh):
    return jax.shard_map(
        on_device,
        mesh=mesh,
        in_specs=(
            P("dp", "rel"),
            P(("dp", "rel"), None),
            P(),
            P("dp", "rel", None),
            P("dp", "rel", None),
            P("dp", "rel"),
            P("rel"),
        ),
        out_specs=(P(("dp", "rel"), None), P(("dp", "rel"), None)),
        check_vma=False,
    )
```

```python
import functools

import jax
import jax.numpy as jnp
from jax import lax
from jax.experimental import pallas as pl
from jax.experimental.pallas import tpu as pltpu
from jax.sharding import PartitionSpec as P

I32 = jnp.int32
BF16 = jnp.bfloat16
F32 = jnp.float32
D_IN = 768
HID = 512
RELS = 5
COLS = RELS * HID
FANOUT = 16
SLOTS = 512
TGT = 1024
BLKS = 8
POOL = 2048
OWN = 256
NO_EDGE = RELS * POOL
PLANES = 10
HALF = COLS // 2
ROWS_OUT = 6
LANES = 128
CHUNK = 64
DEVICES = 128
TILES = TGT // LANES
STEP = 2
PIECE = HID // 8
COST_FIRST = 1_000_000_000
COST_COUNT = 20_000_000_000


def edge_kernel(valid_ref, rel_ref, ids_ref, nbr_ref, out_ref):
    lane = lax.broadcasted_iota(I32, (8, LANES), 1)
    sub = lax.broadcasted_iota(I32, (8, LANES), 0)
    meta = jnp.zeros((8, LANES), I32)
    for b in range(BLKS):
        rel = rel_ref[b]
        limit = valid_ref[0, b]
        meta = jnp.where((sub == b) & (lane == 0), rel, meta)
        meta = jnp.where((sub == b) & (lane == 1), (limit + (STEP * LANES - 1)) // (STEP * LANES), meta)
        node = ids_ref[b : b + 1, :]
        code = rel * POOL + (node & 1792) + ((node & 7) << 5) + ((node >> 3) & 31)
        tables = [
            jnp.broadcast_to(code[:, i * LANES : (i + 1) * LANES], (8, LANES))
            for i in range(SLOTS // LANES)
        ]
        for t in range(TGT // LANES):
            cols = slice(t * LANES, (t + 1) * LANES)
            live = (lane + t * LANES) < limit
            halves = []
            for half in range(2):
                slot = nbr_ref[b, half * 8 : (half + 1) * 8, cols]
                low = slot & (LANES - 1)
                high = slot >> 7
                got = [
                    jnp.take_along_axis(table, low, axis=1, mode="promise_in_bounds")
                    for table in tables
                ]
                found = jnp.where(
                    high < 2,
                    jnp.where(high == 0, got[0], got[1]),
                    jnp.where(high == 2, got[2], got[3]),
                )
                halves.append(jnp.where(live, found, NO_EDGE))
            out_ref[b * TILES + t] = halves[0] | (halves[1] << 16)
    out_ref[BLKS * TILES] = meta


def edge_codes(valid_rows, block_rel, ids, nbr):
    return pl.pallas_call(
        edge_kernel,
        out_shape=jax.ShapeDtypeStruct((BLKS * TILES + 1, 8, LANES), I32),
        in_specs=[pl.BlockSpec(memory_space=pltpu.SMEM)] * 2
        + [pl.BlockSpec(memory_space=pltpu.VMEM)] * 2,
        out_specs=pl.BlockSpec(memory_space=pltpu.VMEM),
        cost_estimate=pl.CostEstimate(flops=0, bytes_accessed=1 << 20, transcendentals=0),
        name="edge_codes",
    )(valid_rows, block_rel, ids, nbr)


def full_add(a, b, c):
    x = a ^ b
    return x ^ c, (a & b) | (c & x)


def count_bits(masks, planes):
    carried = masks
    out = []
    for i in range(PLANES):
        cur = carried + [planes[i]]
        carried = []
        while len(cur) >= 3:
            s, c = full_add(cur[0], cur[1], cur[2])
            cur = cur[3:] + [s]
            carried.append(c)
        if len(cur) == 2:
            carried.append(cur[0] & cur[1])
            cur = [cur[0] ^ cur[1]]
        out.append(cur[0])
    return out


def swap_bits(a, b, shift, mask):
    if a is None and b is None:
        return a, b
    if b is None:
        t = lax.shift_right_logical(a, jnp.int32(shift)) & mask
        return a & mask, t
    t = (lax.shift_right_logical(a, jnp.int32(shift)) ^ b) & mask
    return a ^ (t << shift), b ^ t


def plane_bytes(planes):
    x = list(planes)
    for shift, mask in ((4, 0x0F0F0F0F), (2, 0x33333333), (1, 0x55555555)):
        for i in range(8):
            if not i & shift:
                x[i], x[i + shift] = swap_bits(x[i], x[i + shift], shift, mask)
    return x


def counts(planes):
    low = plane_bytes(planes[:8])
    high = plane_bytes(planes[8:] + [None] * (16 - PLANES))
    pair = 0x00FF00FF
    rows = [None] * 32
    for off in range(8):
        even = (low[off] & pair) | ((high[off] & pair) << 8)
        odd = (lax.shift_right_logical(low[off], jnp.int32(8)) & pair) | (high[off] & ~pair)
        for q, word in enumerate((even, odd)):
            rows[off + 8 * q] = (word & 0xFFFF).astype(F32)
            rows[off + 8 * q + 16] = lax.shift_right_logical(word, jnp.int32(16)).astype(F32)
    return jnp.concatenate(rows, axis=0).astype(BF16)


def start_loads(edges, words, meta, word_sems, meta_sems):
    loads = []
    for i, edge in enumerate(edges):
        m = pltpu.make_async_copy(edge.at[BLKS * TILES], meta.at[i], meta_sems.at[i])
        w = pltpu.make_async_copy(edge.at[pl.ds(0, BLKS * TILES)], words.at[i], word_sems.at[i])
        m.start()
        w.start()
        loads.append((m, w))
    return loads


def count_all(mine, loads, words, meta, keys, planes_ref):
    row = lax.broadcasted_iota(I32, (STEP, 8, LANES), 1)
    for i, load in enumerate(loads):
        for copy in load:
            copy.wait()

        def one_block(b, carry, i=i):
            rel = meta[i, b, 0]
            steps = meta[i, b, 1]
            word = words[i, pl.ds(b * TILES, TILES)]
            for half, code in enumerate((word & 0xFFFF, word >> 16)):
                keys[half, 0] = code >> 5
                keys[half, 1] = jnp.left_shift(jnp.int32(1), code & 31)
            target = row + (rel * (POOL // 32) + mine * (OWN // 32))

            def one_step(t, carry):
                at = pl.ds(t * STEP, STEP)
                masks = []
                for half in range(2):
                    for s in range(8):
                        key = jnp.broadcast_to(keys[half, 0, at, s : s + 1, :], target.shape)
                        bit = jnp.broadcast_to(keys[half, 1, at, s : s + 1, :], target.shape)
                        masks.append(jnp.where(key == target, bit, 0))
                new = count_bits(masks, [planes_ref[rel, p, at] for p in range(PLANES)])
                for p in range(PLANES):
                    planes_ref[rel, p, at] = new[p]
                return carry

            return lax.fori_loop(0, steps, one_step, carry)

        lax.fori_loop(0, BLKS, one_block, 0)


PLANE_SHAPE = (RELS, PLANES, TILES, 8, LANES)


def count_scratch(n):
    return [
        pltpu.VMEM((n, BLKS * TILES, 8, LANES), I32),
        pltpu.VMEM((2, 2, TILES, 8, LANES), I32),
        pltpu.SMEM((n, 8, LANES), I32),
        pltpu.SemaphoreType.DMA((n,)),
        pltpu.SemaphoreType.DMA((n,)),
    ]


def first_kernel(n, place_ref, *refs):
    edges, grads = refs[:n], refs[n : n + 4]
    planes_ref, half_ref = refs[n + 4 : n + 6]
    words, keys, meta, word_sems, meta_sems, grad_sems = refs[n + 6 :]
    loads = start_loads(edges, words, meta, word_sems, meta_sems)
    copies = []
    for k in range(4):
        z = (place_ref[0] // 2 - k) & 3
        rows = pl.ds(pl.multiple_of(z * PIECE, PIECE), PIECE)
        copies.append(pltpu.make_async_copy(grads[k], half_ref.at[rows], grad_sems.at[k]))
        copies[k].start()
    planes_ref[...] = jnp.zeros_like(planes_ref)
    count_all(place_ref[0], loads, words, meta, keys, planes_ref)
    for copy in copies:
        copy.wait()


def count_first(place, edges, grads):
    n = len(edges)
    vmem = pl.BlockSpec(memory_space=pltpu.VMEM)
    return pl.pallas_call(
        functools.partial(first_kernel, n),
        out_shape=[
            jax.ShapeDtypeStruct(PLANE_SHAPE, I32),
            jax.ShapeDtypeStruct((HID // 2, TGT), BF16),
        ],
        in_specs=[pl.BlockSpec(memory_space=pltpu.SMEM)]
        + [pl.BlockSpec(memory_space=pl.ANY)] * (n + 4),
        out_specs=[vmem] * 2,
        scratch_shapes=count_scratch(n) + [pltpu.SemaphoreType.DMA((4,))],
        compiler_params=pltpu.CompilerParams(vmem_limit_bytes=14 << 20),
        cost_estimate=pl.CostEstimate(
            flops=COST_FIRST, bytes_accessed=1 << 20, transcendentals=0
        ),
        name="count_first",
    )(place, *edges, *grads)


def count_kernel(n, place_ref, *refs):
    edges = refs[:n]
    start_ref, planes_ref, words, keys, meta, word_sems, meta_sems = refs[n:]
    loads = start_loads(edges, words, meta, word_sems, meta_sems)
    planes_ref[...] = start_ref[...]
    count_all(place_ref[0], loads, words, meta, keys, planes_ref)


def count_edges(place, edges, planes):
    n = len(edges)
    vmem = pl.BlockSpec(memory_space=pltpu.VMEM)
    return pl.pallas_call(
        functools.partial(count_kernel, n),
        out_shape=jax.ShapeDtypeStruct(PLANE_SHAPE, I32),
        in_specs=[pl.BlockSpec(memory_space=pltpu.SMEM)]
        + [pl.BlockSpec(memory_space=pl.ANY)] * n
        + [vmem],
        out_specs=vmem,
        scratch_shapes=count_scratch(n),
        compiler_params=pltpu.CompilerParams(vmem_limit_bytes=14 << 20),
        cost_estimate=pl.CostEstimate(
            flops=COST_COUNT, bytes_accessed=n << 19, transcendentals=0
        ),
        name="count_edges",
    )(place, *edges, planes)


def hidden_kernel(n, place_ref, *refs):
    edges = refs[:n]
    mine_ref, far_ref, start_ref, own_ref, other_ref = refs[n : n + 5]
    words, keys, meta, word_sems, meta_sems, planes_ref, adj = refs[n + 5 :]
    loads = start_loads(edges, words, meta, word_sems, meta_sems)
    planes_ref[...] = start_ref[...]
    count_all(place_ref[0], loads, words, meta, keys, planes_ref)
    half = HID // 2
    for r in range(RELS):
        for t in range(TILES):
            adj[r % 2, :, t * LANES : (t + 1) * LANES] = counts(
                [planes_ref[r, p, t] for p in range(PLANES)]
            )
        for out_ref, grads_ref in ((other_ref, far_ref), (own_ref, mine_ref)):
            h = lax.dot_general(
                adj[r % 2], grads_ref[...], (((1,), (1,)), ((), ())), preferred_element_type=F32
            )
            out_ref[:, r * half : (r + 1) * half] = (h * (1.0 / FANOUT)).astype(BF16)


def hidden_halves(place, edges, mine, far, planes):
    n = len(edges)
    vmem = pl.BlockSpec(memory_space=pltpu.VMEM)
    return pl.pallas_call(
        functools.partial(hidden_kernel, n),
        out_shape=[jax.ShapeDtypeStruct((OWN, HALF), BF16)] * 2,
        in_specs=[pl.BlockSpec(memory_space=pltpu.SMEM)]
        + [pl.BlockSpec(memory_space=pl.ANY)] * n
        + [vmem] * 3,
        out_specs=[vmem] * 2,
        scratch_shapes=count_scratch(n)
        + [pltpu.VMEM(PLANE_SHAPE, I32), pltpu.VMEM((2, OWN, TGT), BF16)],
        compiler_params=pltpu.CompilerParams(vmem_limit_bytes=18 << 20),
        cost_estimate=pl.CostEstimate(
            flops=8_000_000_000, bytes_accessed=4 << 20, transcendentals=0
        ),
        name="hidden_halves",
    )(place, *edges, mine, far, planes)


def weave(low, high, odd):
    lane = lax.broadcasted_iota(I32, low.shape, 1)
    if odd:
        return jnp.where(lane < LANES // 2, pltpu.roll(low, LANES // 2, 1), high)
    return jnp.where(lane < LANES // 2, low, pltpu.roll(high, LANES // 2, 1))


def source_kernel(place_ref, own_ref, other_ref, weight_ref, out_ref, hidden):
    first = place_ref[1] == 0
    for i in range(HALF // LANES):
        cols = slice(i * LANES, (i + 1) * LANES)
        own, other = own_ref[:, cols].astype(F32), other_ref[:, cols].astype(F32)
        low, high = jnp.where(first, own, other), jnp.where(first, other, own)
        for odd in range(2):
            to = (2 * i + odd) * LANES
            hidden[:, to : to + LANES] = weave(low, high, odd).astype(BF16)
    out_ref[...] = lax.dot_general(
        hidden[...], weight_ref[...], (((1,), (1,)), ((), ())), preferred_element_type=F32
    ).astype(BF16)


def source_rows(place, own, other, weight):
    vmem = pl.BlockSpec(memory_space=pltpu.VMEM)
    return pl.pallas_call(
        source_kernel,
        out_shape=jax.ShapeDtypeStruct((OWN, D_IN), BF16),
        in_specs=[pl.BlockSpec(memory_space=pltpu.SMEM)] + [vmem] * 3,
        out_specs=vmem,
        scratch_shapes=[pltpu.VMEM((OWN, COLS), BF16)],
        compiler_params=pltpu.CompilerParams(vmem_limit_bytes=16 << 20),
        cost_estimate=pl.CostEstimate(
            flops=1_000_000_000, bytes_accessed=6 << 20, transcendentals=0
        ),
        name="source_rows",
    )(place, own, other, weight)


def product_kernel(h0_ref, h1_ref, f0_ref, f1_ref, out_ref, chunks, packed, sems):
    tiles = HALF // LANES
    chunks[:, ROWS_OUT * tiles :, :] = jnp.zeros((DEVICES, CHUNK - ROWS_OUT * tiles, LANES), F32)
    for r in range(ROWS_OUT):
        rows = slice(r * LANES, (r + 1) * LANES)
        p = jnp.dot(f0_ref[rows, :], h0_ref[...], preferred_element_type=F32)
        p += jnp.dot(f1_ref[rows, :], h1_ref[...], preferred_element_type=F32)
        for c in range(tiles):
            chunks[:, r * tiles + c, :] = p[:, c * LANES : (c + 1) * LANES]
    step = DEVICES // 4
    copies = []
    for i in range(4):
        part = pl.ds(i * step, step)
        packed[part] = chunks[part].astype(BF16)
        copies.append(pltpu.make_async_copy(packed.at[part], out_ref.at[part], sems.at[i]))
        copies[i].start()
    for copy in copies:
        copy.wait()


def products(h0, h1, f0, f1):
    vmem = pl.BlockSpec(memory_space=pltpu.VMEM)
    return pl.pallas_call(
        product_kernel,
        out_shape=jax.ShapeDtypeStruct((DEVICES, CHUNK, LANES), BF16),
        in_specs=[vmem] * 4,
        out_specs=pl.BlockSpec(memory_space=pltpu.HBM),
        scratch_shapes=[
            pltpu.VMEM((DEVICES, CHUNK, LANES), F32),
            pltpu.VMEM((DEVICES, CHUNK, LANES), BF16),
            pltpu.SemaphoreType.DMA((4,)),
        ],
        compiler_params=pltpu.CompilerParams(vmem_limit_bytes=24 << 20),
        cost_estimate=pl.CostEstimate(
            flops=1_000_000_000, bytes_accessed=5 << 20, transcendentals=0
        ),
        name="products",
    )(h0, h1, f0, f1)


def sum_kernel(scale, got_ref, out_ref, sums):
    tiles = HALF // LANES
    totals = [None, None]
    for d in range(DEVICES):
        term = got_ref[d].astype(F32)
        core = d % 2
        totals[core] = term if totals[core] is None else totals[core] + term
    for odd in range(2):
        sums[odd] = weave(totals[0] * scale, totals[1] * scale, odd)
    for r in range(ROWS_OUT):
        for i in range(tiles):
            for odd in range(2):
                to = (2 * i + odd) * LANES
                at = r * tiles + i
                out_ref[r : r + 1, to : to + LANES] = sums[odd, at : at + 1, :]


def sum_chunks(got, scale):
    vmem = pl.BlockSpec(memory_space=pltpu.VMEM)
    return pl.pallas_call(
        functools.partial(sum_kernel, scale),
        out_shape=jax.ShapeDtypeStruct((ROWS_OUT, COLS), F32),
        in_specs=[vmem],
        out_specs=vmem,
        scratch_shapes=[pltpu.VMEM((2, CHUNK, LANES), F32)],
        compiler_params=pltpu.CompilerParams(vmem_limit_bytes=14 << 20),
        cost_estimate=pl.CostEstimate(flops=1 << 20, bytes_accessed=2 << 20, transcendentals=0),
        name="sum_chunks",
    )(got)


def on_device(grad_out, src_feat, weight, nbr_slot, src_ids, valid_rows, block_rel):
    rel = lax.axis_index("rel")
    place = jnp.stack([rel, rel & 1]).astype(I32)

    def along_z(v, k):
        return lax.ppermute(v, "rel", [(i, (i + 2 * k) % 8) for i in range(8)])

    def other_core(v):
        return lax.ppermute(v, "rel", [(i, i ^ 1) for i in range(8)])

    codes = edge_codes(valid_rows, block_rel, src_ids[0], nbr_slot.transpose(1, 2, 0))
    far = {k: along_z(codes, k) for k in (2, 1, 3)}
    grads = [grad_out.T]
    grads += [along_z(grads[0], k) for k in (1, 2, 3)]
    planes, mine = count_first(place, [codes, other_core(codes)], grads)
    planes = count_edges(place, [far[k] for k in (2, 1, 3)], planes)

    old = jnp.arange(D_IN, dtype=I32)[:, None]
    new = jnp.arange(D_IN, dtype=I32)[None, :]
    order = (old == (new % LANES) * ROWS_OUT + new // LANES).astype(BF16)
    feats = lax.dot_general(
        order, src_feat, (((0,), (1,)), ((), ())), preferred_element_type=F32
    ).astype(BF16)
    feats_other = other_core(feats)

    swapped = [other_core(far[k]) for k in (2, 1, 3)]
    own, other = hidden_halves(place, swapped, mine, other_core(mine), planes)
    got = other_core(other)
    source_grad = source_rows(place, own, other, weight)
    chunks = products(own, got, feats, feats_other)
    chunks = lax.all_to_all(chunks, ("dp", "rel"), 0, 0, tiled=True)
    return source_grad, sum_chunks(chunks, float(TGT * 16) ** (-0.5))


def solution(mesh):
    return jax.shard_map(
        on_device,
        mesh=mesh,
        in_specs=(
            P("dp", "rel"),
            P(("dp", "rel"), None),
            P(),
            P("dp", "rel", None),
            P("dp", "rel", None),
            P("dp", "rel"),
            P("rel"),
        ),
        out_specs=(P(("dp", "rel"), None), P(("dp", "rel"), None)),
        check_vma=False,
    )
```

```python
import functools

import jax
import jax.numpy as jnp
from jax import lax
from jax.experimental import pallas as pl
from jax.experimental.pallas import tpu as pltpu
from jax.sharding import PartitionSpec as P

I32 = jnp.int32
BF16 = jnp.bfloat16
F32 = jnp.float32
D_IN = 768
HID = 512
RELS = 5
COLS = RELS * HID
FANOUT = 16
SLOTS = 512
TGT = 1024
BLKS = 8
POOL = 2048
OWN = 256
NO_EDGE = RELS * POOL
PLANES = 10
ROWS_OUT = 6
LANES = 128
CHUNK = 120
PEERS = 64
PRODUCT_VMEM = 24
TILES = TGT // LANES
STEP = 2
PIECE = HID // 8


def edge_kernel(valid_ref, rel_ref, ids_ref, nbr_ref, out_ref):
    lane = lax.broadcasted_iota(I32, (8, LANES), 1)
    sub = lax.broadcasted_iota(I32, (8, LANES), 0)
    meta = jnp.zeros((8, LANES), I32)
    for b in range(BLKS):
        rel = rel_ref[b]
        limit = valid_ref[0, b]
        meta = jnp.where((sub == b) & (lane == 0), rel, meta)
        meta = jnp.where((sub == b) & (lane == 1), (limit + (STEP * LANES - 1)) // (STEP * LANES), meta)
        node = ids_ref[b : b + 1, :]
        code = rel * POOL + (node & 1792) + ((node & 7) << 5) + ((node >> 3) & 31)
        tables = [
            jnp.broadcast_to(code[:, i * LANES : (i + 1) * LANES], (8, LANES))
            for i in range(SLOTS // LANES)
        ]
        for t in range(TGT // LANES):
            cols = slice(t * LANES, (t + 1) * LANES)
            live = (lane + t * LANES) < limit
            halves = []
            for half in range(2):
                slot = nbr_ref[b, half * 8 : (half + 1) * 8, cols]
                low = slot & (LANES - 1)
                high = slot >> 7
                got = [
                    jnp.take_along_axis(table, low, axis=1, mode="promise_in_bounds")
                    for table in tables
                ]
                found = jnp.where(
                    high < 2,
                    jnp.where(high == 0, got[0], got[1]),
                    jnp.where(high == 2, got[2], got[3]),
                )
                halves.append(jnp.where(live, found, NO_EDGE))
            out_ref[b * TILES + t] = halves[0] | (halves[1] << 16)
    out_ref[BLKS * TILES] = meta


def edge_codes(valid_rows, block_rel, ids, nbr):
    return pl.pallas_call(
        edge_kernel,
        out_shape=jax.ShapeDtypeStruct((BLKS * TILES + 1, 8, LANES), I32),
        in_specs=[pl.BlockSpec(memory_space=pltpu.SMEM)] * 2
        + [pl.BlockSpec(memory_space=pltpu.VMEM)] * 2,
        out_specs=pl.BlockSpec(memory_space=pltpu.VMEM),
        cost_estimate=pl.CostEstimate(flops=0, bytes_accessed=1 << 20, transcendentals=0),
        name="edge_codes",
    )(valid_rows, block_rel, ids, nbr)


def full_add(a, b, c):
    x = a ^ b
    return x ^ c, (a & b) | (c & x)


def count_bits(masks, planes):
    carried = masks
    out = []
    for i in range(PLANES):
        cur = carried + [planes[i]]
        carried = []
        while len(cur) >= 3:
            s, c = full_add(cur[0], cur[1], cur[2])
            cur = cur[3:] + [s]
            carried.append(c)
        if len(cur) == 2:
            carried.append(cur[0] & cur[1])
            cur = [cur[0] ^ cur[1]]
        out.append(cur[0])
    return out


def swap_bits(a, b, shift, mask):
    if a is None and b is None:
        return a, b
    if b is None:
        t = lax.shift_right_logical(a, jnp.int32(shift)) & mask
        return a & mask, t
    t = (lax.shift_right_logical(a, jnp.int32(shift)) ^ b) & mask
    return a ^ (t << shift), b ^ t


def plane_bytes(planes):
    x = list(planes)
    for shift, mask in ((4, 0x0F0F0F0F), (2, 0x33333333), (1, 0x55555555)):
        for i in range(8):
            if not i & shift:
                x[i], x[i + shift] = swap_bits(x[i], x[i + shift], shift, mask)
    return x


def counts(planes):
    low = plane_bytes(planes[:8])
    high = plane_bytes(planes[8:] + [None] * (16 - PLANES))
    pair = 0x00FF00FF
    rows = [None] * 32
    for off in range(8):
        even = (low[off] & pair) | ((high[off] & pair) << 8)
        odd = (lax.shift_right_logical(low[off], jnp.int32(8)) & pair) | (high[off] & ~pair)
        for q, word in enumerate((even, odd)):
            rows[off + 8 * q] = (word & 0xFFFF).astype(F32)
            rows[off + 8 * q + 16] = lax.shift_right_logical(word, jnp.int32(16)).astype(F32)
    return jnp.concatenate(rows, axis=0).astype(BF16)


def start_loads(edges, words, meta, word_sems, meta_sems):
    loads = []
    for i, edge in enumerate(edges):
        m = pltpu.make_async_copy(edge.at[BLKS * TILES], meta.at[i], meta_sems.at[i])
        w = pltpu.make_async_copy(edge.at[pl.ds(0, BLKS * TILES)], words.at[i], word_sems.at[i])
        m.start()
        w.start()
        loads.append((m, w))
    return loads


def count_all(mine, loads, words, meta, keys, planes_ref):
    row = lax.broadcasted_iota(I32, (STEP, 8, LANES), 1)
    for i, load in enumerate(loads):
        for copy in load:
            copy.wait()

        def one_block(b, carry, i=i):
            rel = meta[i, b, 0]
            steps = meta[i, b, 1]
            word = words[i, pl.ds(b * TILES, TILES)]
            for half, code in enumerate((word & 0xFFFF, word >> 16)):
                keys[half, 0] = code >> 5
                keys[half, 1] = jnp.left_shift(jnp.int32(1), code & 31)
            target = row + (rel * (POOL // 32) + mine * (OWN // 32))

            def one_step(t, carry):
                at = pl.ds(t * STEP, STEP)
                masks = []
                for half in range(2):
                    for s in range(8):
                        key = jnp.broadcast_to(keys[half, 0, at, s : s + 1, :], target.shape)
                        bit = jnp.broadcast_to(keys[half, 1, at, s : s + 1, :], target.shape)
                        masks.append(jnp.where(key == target, bit, 0))
                new = count_bits(masks, [planes_ref[rel, p, at] for p in range(PLANES)])
                for p in range(PLANES):
                    planes_ref[rel, p, at] = new[p]
                return carry

            return lax.fori_loop(0, steps, one_step, carry)

        lax.fori_loop(0, BLKS, one_block, 0)


PLANE_SHAPE = (RELS, PLANES, TILES, 8, LANES)


def count_scratch(n):
    return [
        pltpu.VMEM((n, BLKS * TILES, 8, LANES), I32),
        pltpu.VMEM((2, 2, TILES, 8, LANES), I32),
        pltpu.SMEM((n, 8, LANES), I32),
        pltpu.SemaphoreType.DMA((n,)),
        pltpu.SemaphoreType.DMA((n,)),
    ]


def count_kernel(n, place_ref, *refs):
    edges = refs[:n]
    planes_ref, words, keys, meta, word_sems, meta_sems = refs[n + 1 :]
    loads = start_loads(edges, words, meta, word_sems, meta_sems)
    planes_ref[...] = refs[n][...]
    count_all(place_ref[0], loads, words, meta, keys, planes_ref)


def first_kernel(place_ref, edge_ref, *refs):
    grads = refs[:4]
    planes_ref, half_ref, words, keys, meta, word_sems, meta_sems, grad_sems = refs[4:]
    loads = start_loads([edge_ref], words, meta, word_sems, meta_sems)
    copies = []
    for k in range(4):
        z = (place_ref[0] // 2 - k) & 3
        rows = pl.ds(pl.multiple_of(z * PIECE, PIECE), PIECE)
        copies.append(pltpu.make_async_copy(grads[k], half_ref.at[rows], grad_sems.at[k]))
        copies[k].start()
    planes_ref[...] = jnp.zeros_like(planes_ref)
    count_all(place_ref[0], loads, words, meta, keys, planes_ref)
    for copy in copies:
        copy.wait()


def count_first(place, edge, grads):
    vmem = pl.BlockSpec(memory_space=pltpu.VMEM)
    return pl.pallas_call(
        first_kernel,
        out_shape=[
            jax.ShapeDtypeStruct(PLANE_SHAPE, I32),
            jax.ShapeDtypeStruct((HID // 2, TGT), BF16),
        ],
        in_specs=[pl.BlockSpec(memory_space=pltpu.SMEM)]
        + [pl.BlockSpec(memory_space=pl.ANY)] * 5,
        out_specs=[vmem] * 2,
        scratch_shapes=count_scratch(1) + [pltpu.SemaphoreType.DMA((4,))],
        compiler_params=pltpu.CompilerParams(vmem_limit_bytes=14 << 20),
        cost_estimate=pl.CostEstimate(
            flops=2_000_000_000, bytes_accessed=1 << 20, transcendentals=0
        ),
        name="count_first",
    )(place, edge, *grads)


def count_edges(place, edges, planes):
    n = len(edges)
    vmem = pl.BlockSpec(memory_space=pltpu.VMEM)
    return pl.pallas_call(
        functools.partial(count_kernel, n),
        out_shape=jax.ShapeDtypeStruct(PLANE_SHAPE, I32),
        in_specs=[pl.BlockSpec(memory_space=pltpu.SMEM)]
        + [pl.BlockSpec(memory_space=pl.ANY)] * n
        + [vmem],
        out_specs=vmem,
        scratch_shapes=count_scratch(n),
        compiler_params=pltpu.CompilerParams(vmem_limit_bytes=14 << 20),
        cost_estimate=pl.CostEstimate(
            flops=n * 1_500_000_000, bytes_accessed=n << 19, transcendentals=0
        ),
        name="count_edges",
    )(place, *edges, planes)


def after_kernel(value_ref, earlier_ref, out_ref):
    pass


def after(value, earlier):
    anywhere = pl.BlockSpec(memory_space=pl.ANY)
    return pl.pallas_call(
        after_kernel,
        out_shape=jax.ShapeDtypeStruct(value.shape, value.dtype),
        in_specs=[anywhere] * 2,
        out_specs=anywhere,
        input_output_aliases={0: 0},
        compiler_params=pltpu.CompilerParams(vmem_limit_bytes=1 << 20),
        name="after",
    )(value, earlier)


def hidden_kernel(place_ref, mine_ref, far_ref, planes_ref, out_ref, adj, grads_vmem, sems):
    copies = []
    for i in range(8):
        core = place_ref[1] if i < 4 else 1 - place_ref[1]
        half = mine_ref if i < 4 else far_ref
        rows = pl.ds(pl.multiple_of((i % 4 * 2 + core) * PIECE, PIECE), PIECE)
        piece = half.at[pl.ds(i % 4 * PIECE, PIECE)]
        copies.append(pltpu.make_async_copy(piece, grads_vmem.at[rows], sems.at[i]))
        copies[i].start()
    for r in range(RELS):
        for t in range(TILES):
            adj[r % 2, :, t * LANES : (t + 1) * LANES] = counts(
                [planes_ref[r, p, t] for p in range(PLANES)]
            )
        if r == 0:
            for copy in copies:
                copy.wait()
        h = lax.dot_general(
            adj[r % 2], grads_vmem[...], (((1,), (1,)), ((), ())), preferred_element_type=F32
        )
        out_ref[:, r * HID : (r + 1) * HID] = (h * (1.0 / FANOUT)).astype(BF16)


def hidden_rows(place, mine, far, planes):
    vmem = pl.BlockSpec(memory_space=pltpu.VMEM)
    return pl.pallas_call(
        hidden_kernel,
        out_shape=jax.ShapeDtypeStruct((OWN, COLS), BF16),
        in_specs=[pl.BlockSpec(memory_space=pltpu.SMEM)]
        + [pl.BlockSpec(memory_space=pl.ANY)] * 2
        + [vmem],
        out_specs=vmem,
        scratch_shapes=[
            pltpu.VMEM((2, OWN, TGT), BF16),
            pltpu.VMEM((HID, TGT), BF16),
            pltpu.SemaphoreType.DMA((8,)),
        ],
        compiler_params=pltpu.CompilerParams(vmem_limit_bytes=14 << 20),
        cost_estimate=pl.CostEstimate(
            flops=3_000_000_000, bytes_accessed=4 << 20, transcendentals=0
        ),
        name="hidden_rows",
    )(place, mine, far, planes)


def source_kernel(hidden_ref, weight_ref, out_ref):
    out_ref[...] = lax.dot_general(
        hidden_ref[...], weight_ref[...], (((1,), (1,)), ((), ())), preferred_element_type=F32
    ).astype(BF16)


def source_rows(hidden, weight):
    vmem = pl.BlockSpec(memory_space=pltpu.VMEM)
    return pl.pallas_call(
        source_kernel,
        out_shape=jax.ShapeDtypeStruct((OWN, D_IN), BF16),
        in_specs=[vmem] * 2,
        out_specs=vmem,
        compiler_params=pltpu.CompilerParams(vmem_limit_bytes=16 << 20),
        cost_estimate=pl.CostEstimate(
            flops=1_000_000_000, bytes_accessed=6 << 20, transcendentals=0
        ),
        name="source_rows",
    )(hidden, weight)


def product_kernel(h0_ref, h1_ref, f0_ref, f1_ref, out_ref, chunks):
    tiles = COLS // LANES
    for r in range(ROWS_OUT):
        rows = slice(r * PEERS, (r + 1) * PEERS)
        p = jnp.dot(f0_ref[rows, :], h0_ref[...], preferred_element_type=F32)
        p += jnp.dot(f1_ref[rows, :], h1_ref[...], preferred_element_type=F32)
        for c in range(tiles):
            chunks[:, r * tiles + c, :] = p[:, c * LANES : (c + 1) * LANES]
    out_ref[...] = chunks[...].astype(BF16)


def products(h0, h1, f0, f1):
    vmem = pl.BlockSpec(memory_space=pltpu.VMEM)
    return pl.pallas_call(
        product_kernel,
        out_shape=jax.ShapeDtypeStruct((PEERS, CHUNK, LANES), BF16),
        in_specs=[vmem] * 4,
        out_specs=vmem,
        scratch_shapes=[pltpu.VMEM((PEERS, CHUNK, LANES), F32)],
        compiler_params=pltpu.CompilerParams(vmem_limit_bytes=PRODUCT_VMEM << 20),
        cost_estimate=pl.CostEstimate(
            flops=1_000_000_000, bytes_accessed=5 << 20, transcendentals=0
        ),
        name="products",
    )(h0, h1, f0, f1)


def sum_kernel(scale, got_ref, out_ref, sums):
    tiles = COLS // LANES
    total = got_ref[0].astype(F32)
    for d in range(1, PEERS):
        total += got_ref[d].astype(F32)
    sums[...] = total * scale
    for r in range(ROWS_OUT):
        for i in range(tiles):
            at = r * tiles + i
            out_ref[r : r + 1, i * LANES : (i + 1) * LANES] = sums[at : at + 1, :]


def sum_chunks(got, scale):
    vmem = pl.BlockSpec(memory_space=pltpu.VMEM)
    return pl.pallas_call(
        functools.partial(sum_kernel, scale),
        out_shape=jax.ShapeDtypeStruct((ROWS_OUT, COLS), F32),
        in_specs=[vmem],
        out_specs=vmem,
        scratch_shapes=[pltpu.VMEM((CHUNK, LANES), F32)],
        compiler_params=pltpu.CompilerParams(vmem_limit_bytes=14 << 20),
        cost_estimate=pl.CostEstimate(flops=1 << 20, bytes_accessed=2 << 20, transcendentals=0),
        name="sum_chunks",
    )(got)


def on_device(grad_out, src_feat, weight, nbr_slot, src_ids, valid_rows, block_rel):
    rel = lax.axis_index("rel")
    core = rel & 1
    place = jnp.stack([rel, core]).astype(I32)

    def along_z(v, k):
        return lax.ppermute(v, "rel", [(i, (i + 2 * k) % 8) for i in range(8)])

    def other_core(v):
        return lax.ppermute(v, "rel", [(i, i ^ 1) for i in range(8)])

    codes = edge_codes(valid_rows, block_rel, src_ids[0], nbr_slot.transpose(1, 2, 0))
    far = {k: along_z(codes, k) for k in (1, 3, 2)}
    grads = {0: grad_out.T}
    for k in (1, 3, 2):
        grads[k] = along_z(grads[0], k)
    planes, mine = count_first(place, codes, [grads[k] for k in range(4)])
    planes = count_edges(place, [other_core(codes), far[1], far[3]], planes)
    planes = count_edges(place, [other_core(far[1]), other_core(far[3])], planes)
    last = after(far[2], planes)
    planes = count_edges(place, [last], planes)
    planes = count_edges(place, [other_core(last)], planes)

    old = jnp.arange(D_IN, dtype=I32)[:, None]
    new = jnp.arange(D_IN // 2, dtype=I32)[None, :]

    def half_feats(which):
        device = (new % PEERS) * 2 + which
        order = (old == device * ROWS_OUT + new // PEERS).astype(BF16)
        return lax.dot_general(
            order, src_feat, (((0,), (1,)), ((), ())), preferred_element_type=F32
        ).astype(BF16)

    feats = half_feats(core)
    feats_other = other_core(half_feats(1 - core))

    hidden = hidden_rows(place, mine, other_core(mine), planes)
    got = other_core(hidden)
    source_grad = source_rows(hidden, weight)
    chunks = products(hidden, got, feats, feats_other)
    groups = [[2 * i + c for i in range(PEERS)] for c in range(2)]
    chunks = lax.all_to_all(
        chunks, ("dp", "rel"), 0, 0, tiled=True, axis_index_groups=groups
    )
    return source_grad, sum_chunks(chunks, float(TGT * 16) ** (-0.5))


def solution(mesh):
    return jax.shard_map(
        on_device,
        mesh=mesh,
        in_specs=(
            P("dp", "rel"),
            P(("dp", "rel"), None),
            P(),
            P("dp", "rel", None),
            P("dp", "rel", None),
            P("dp", "rel"),
            P("rel"),
        ),
        out_specs=(P(("dp", "rel"), None), P(("dp", "rel"), None)),
        check_vma=False,
    )
```

```python
import functools

import jax
import jax.numpy as jnp
from jax import lax
from jax.experimental import pallas as pl
from jax.experimental.pallas import tpu as pltpu
from jax.sharding import PartitionSpec as P

I32 = jnp.int32
BF16 = jnp.bfloat16
F32 = jnp.float32
D_IN = 768
HID = 512
RELS = 5
COLS = RELS * HID
FANOUT = 16
SLOTS = 512
TGT = 1024
BLKS = 8
POOL = 2048
OWN = 256
NO_EDGE = RELS * POOL
PLANES = 10
ROWS_OUT = 6
LANES = 128
CHUNK = 120
PEERS = 64
HALF = COLS // 2
TILES = TGT // LANES
STEP = 2
PIECE = HID // 8
COST_EDGES = 1_000_000
COST_LAST = 1_000_000


def edge_kernel(valid_ref, rel_ref, ids_ref, nbr_ref, grads_ref, out_ref, copy_ref, sem):
    copy = pltpu.make_async_copy(grads_ref, copy_ref, sem)
    copy.start()
    lane = lax.broadcasted_iota(I32, (8, LANES), 1)
    sub = lax.broadcasted_iota(I32, (8, LANES), 0)
    meta = jnp.zeros((8, LANES), I32)
    for b in range(BLKS):
        rel = rel_ref[b]
        limit = valid_ref[0, b]
        meta = jnp.where((sub == b) & (lane == 0), rel, meta)
        meta = jnp.where((sub == b) & (lane == 1), (limit + (STEP * LANES - 1)) // (STEP * LANES), meta)
        node = ids_ref[b : b + 1, :]
        code = rel * POOL + (node & 1792) + ((node & 7) << 5) + ((node >> 3) & 31)
        tables = [
            jnp.broadcast_to(code[:, i * LANES : (i + 1) * LANES], (8, LANES))
            for i in range(SLOTS // LANES)
        ]
        for t in range(TGT // LANES):
            cols = slice(t * LANES, (t + 1) * LANES)
            live = (lane + t * LANES) < limit
            halves = []
            for half in range(2):
                slot = nbr_ref[b, half * 8 : (half + 1) * 8, cols]
                low = slot & (LANES - 1)
                high = slot >> 7
                got = [
                    jnp.take_along_axis(table, low, axis=1, mode="promise_in_bounds")
                    for table in tables
                ]
                found = jnp.where(
                    high < 2,
                    jnp.where(high == 0, got[0], got[1]),
                    jnp.where(high == 2, got[2], got[3]),
                )
                halves.append(jnp.where(live, found, NO_EDGE))
            out_ref[b * TILES + t] = halves[0] | (halves[1] << 16)
    out_ref[BLKS * TILES] = meta
    copy.wait()


def edge_codes(valid_rows, block_rel, ids, nbr, grads):
    anywhere = pl.BlockSpec(memory_space=pl.ANY)
    return pl.pallas_call(
        edge_kernel,
        out_shape=[
            jax.ShapeDtypeStruct((BLKS * TILES + 1, 8, LANES), I32),
            jax.ShapeDtypeStruct(grads.shape, grads.dtype),
        ],
        in_specs=[pl.BlockSpec(memory_space=pltpu.SMEM)] * 2
        + [pl.BlockSpec(memory_space=pltpu.VMEM)] * 2
        + [anywhere],
        out_specs=[pl.BlockSpec(memory_space=pltpu.VMEM), anywhere],
        scratch_shapes=[pltpu.SemaphoreType.DMA],
        cost_estimate=pl.CostEstimate(flops=0, bytes_accessed=1 << 20, transcendentals=0),
        name="edge_codes",
    )(valid_rows, block_rel, ids, nbr, grads)


def full_add(a, b, c):
    x = a ^ b
    return x ^ c, (a & b) | (c & x)


def count_bits(masks, planes):
    carried = masks
    out = []
    for i in range(PLANES):
        cur = carried + [planes[i]]
        carried = []
        while len(cur) >= 3:
            s, c = full_add(cur[0], cur[1], cur[2])
            cur = cur[3:] + [s]
            carried.append(c)
        if len(cur) == 2:
            carried.append(cur[0] & cur[1])
            cur = [cur[0] ^ cur[1]]
        out.append(cur[0])
    return out


def swap_bits(a, b, shift, mask):
    if a is None and b is None:
        return a, b
    if b is None:
        t = lax.shift_right_logical(a, jnp.int32(shift)) & mask
        return a & mask, t
    t = (lax.shift_right_logical(a, jnp.int32(shift)) ^ b) & mask
    return a ^ (t << shift), b ^ t


def plane_bytes(planes):
    x = list(planes)
    for shift, mask in ((4, 0x0F0F0F0F), (2, 0x33333333), (1, 0x55555555)):
        for i in range(8):
            if not i & shift:
                x[i], x[i + shift] = swap_bits(x[i], x[i + shift], shift, mask)
    return x


def counts(planes):
    low = plane_bytes(planes[:8])
    high = plane_bytes(planes[8:] + [None] * (16 - PLANES))
    pair = 0x00FF00FF
    rows = [None] * 32
    for off in range(8):
        even = (low[off] & pair) | ((high[off] & pair) << 8)
        odd = (lax.shift_right_logical(low[off], jnp.int32(8)) & pair) | (high[off] & ~pair)
        for q, word in enumerate((even, odd)):
            rows[off + 8 * q] = (word & 0xFFFF).astype(F32)
            rows[off + 8 * q + 16] = lax.shift_right_logical(word, jnp.int32(16)).astype(F32)
    return jnp.concatenate(rows, axis=0).astype(BF16)


def start_loads(edges, words, meta, word_sems, meta_sems):
    loads = []
    for i, edge in enumerate(edges):
        m = pltpu.make_async_copy(edge.at[BLKS * TILES], meta.at[i], meta_sems.at[i])
        w = pltpu.make_async_copy(edge.at[pl.ds(0, BLKS * TILES)], words.at[i], word_sems.at[i])
        m.start()
        w.start()
        loads.append((m, w))
    return loads


def count_all(mine, loads, words, meta, keys, planes_ref):
    row = lax.broadcasted_iota(I32, (STEP, 8, LANES), 1)
    for i, load in enumerate(loads):
        for copy in load:
            copy.wait()

        def one_block(b, carry, i=i):
            rel = meta[i, b, 0]
            steps = meta[i, b, 1]
            word = words[i, pl.ds(b * TILES, TILES)]
            for half, code in enumerate((word & 0xFFFF, word >> 16)):
                keys[half, 0] = code >> 5
                keys[half, 1] = jnp.left_shift(jnp.int32(1), code & 31)
            target = row + (rel * (POOL // 32) + mine * (OWN // 32))

            def one_step(t, carry):
                at = pl.ds(t * STEP, STEP)
                masks = []
                for half in range(2):
                    for s in range(8):
                        key = jnp.broadcast_to(keys[half, 0, at, s : s + 1, :], target.shape)
                        bit = jnp.broadcast_to(keys[half, 1, at, s : s + 1, :], target.shape)
                        masks.append(jnp.where(key == target, bit, 0))
                new = count_bits(masks, [planes_ref[rel, p, at] for p in range(PLANES)])
                for p in range(PLANES):
                    planes_ref[rel, p, at] = new[p]
                return carry

            return lax.fori_loop(0, steps, one_step, carry)

        lax.fori_loop(0, BLKS, one_block, 0)


PLANE_SHAPE = (RELS, PLANES, TILES, 8, LANES)


def count_scratch(n):
    return [
        pltpu.VMEM((n, BLKS * TILES, 8, LANES), I32),
        pltpu.VMEM((2, 2, TILES, 8, LANES), I32),
        pltpu.SMEM((n, 8, LANES), I32),
        pltpu.SemaphoreType.DMA((n,)),
        pltpu.SemaphoreType.DMA((n,)),
    ]


def count_kernel(n, place_ref, *refs):
    edges = refs[:n]
    planes_ref, words, keys, meta, word_sems, meta_sems = refs[n + 1 :]
    loads = start_loads(edges, words, meta, word_sems, meta_sems)
    planes_ref[...] = refs[n][...]
    count_all(place_ref[0], loads, words, meta, keys, planes_ref)


def first_kernel(place_ref, edge_ref, planes_ref, words, keys, meta, word_sems, meta_sems):
    loads = start_loads([edge_ref], words, meta, word_sems, meta_sems)
    planes_ref[...] = jnp.zeros_like(planes_ref)
    count_all(place_ref[0], loads, words, meta, keys, planes_ref)


def count_first(place, edge):
    return pl.pallas_call(
        first_kernel,
        out_shape=jax.ShapeDtypeStruct(PLANE_SHAPE, I32),
        in_specs=[
            pl.BlockSpec(memory_space=pltpu.SMEM),
            pl.BlockSpec(memory_space=pl.ANY),
        ],
        out_specs=pl.BlockSpec(memory_space=pltpu.VMEM),
        scratch_shapes=count_scratch(1),
        compiler_params=pltpu.CompilerParams(vmem_limit_bytes=14 << 20),
        cost_estimate=pl.CostEstimate(
            flops=2_000_000_000, bytes_accessed=1 << 20, transcendentals=0
        ),
        name="count_first",
    )(place, edge)


def count_edges(place, edges, planes):
    n = len(edges)
    vmem = pl.BlockSpec(memory_space=pltpu.VMEM)
    return pl.pallas_call(
        functools.partial(count_kernel, n),
        out_shape=jax.ShapeDtypeStruct(PLANE_SHAPE, I32),
        in_specs=[pl.BlockSpec(memory_space=pltpu.SMEM)]
        + [pl.BlockSpec(memory_space=pl.ANY)] * n
        + [vmem],
        out_specs=vmem,
        scratch_shapes=count_scratch(n),
        compiler_params=pltpu.CompilerParams(vmem_limit_bytes=14 << 20),
        cost_estimate=pl.CostEstimate(
            flops=n * COST_EDGES, bytes_accessed=1 << 10, transcendentals=0
        ),
        name="count_edges",
    )(place, *edges, planes)


def last_kernel(place_ref, edge_ref, start_ref, adj_ref, *scratch):
    words, keys, meta, word_sems, meta_sems, planes_ref = scratch
    loads = start_loads([edge_ref], words, meta, word_sems, meta_sems)
    planes_ref[...] = start_ref[...]
    count_all(place_ref[0], loads, words, meta, keys, planes_ref)
    for r in range(RELS):
        for t in range(TILES):
            adj_ref[r, :, t * LANES : (t + 1) * LANES] = counts(
                [planes_ref[r, p, t] for p in range(PLANES)]
            )


def count_last(place, edge, planes):
    vmem = pl.BlockSpec(memory_space=pltpu.VMEM)
    return pl.pallas_call(
        last_kernel,
        out_shape=jax.ShapeDtypeStruct((RELS, OWN, TGT), BF16),
        in_specs=[
            pl.BlockSpec(memory_space=pltpu.SMEM),
            pl.BlockSpec(memory_space=pl.ANY),
            vmem,
        ],
        out_specs=vmem,
        scratch_shapes=count_scratch(1) + [pltpu.VMEM(PLANE_SHAPE, I32)],
        compiler_params=pltpu.CompilerParams(vmem_limit_bytes=14 << 20),
        cost_estimate=pl.CostEstimate(
            flops=COST_LAST, bytes_accessed=1 << 10, transcendentals=0
        ),
        name="count_last",
    )(place, edge, planes)


def after_kernel(*refs):
    pass


def after(values, earlier):
    n = len(values)
    anywhere = pl.BlockSpec(memory_space=pl.ANY)
    return pl.pallas_call(
        after_kernel,
        out_shape=[jax.ShapeDtypeStruct(v.shape, v.dtype) for v in values],
        in_specs=[anywhere] * (n + 1),
        out_specs=[anywhere] * n,
        input_output_aliases={i: i for i in range(n)},
        compiler_params=pltpu.CompilerParams(vmem_limit_bytes=1 << 20),
        cost_estimate=pl.CostEstimate(flops=1000, bytes_accessed=1 << 10, transcendentals=0),
        name="after",
    )(*values, earlier)


def hidden_kernel(place_ref, *refs):
    grads = refs[:4]
    adj_ref, out_ref, grads_vmem, sems = refs[4:]
    copies = []
    for k in range(4):
        z = (place_ref[0] // 2 - k) & 3
        rows = pl.ds(pl.multiple_of(z * PIECE, PIECE), PIECE)
        copies.append(pltpu.make_async_copy(grads[k], grads_vmem.at[rows], sems.at[k]))
        copies[k].start()
    for copy in copies:
        copy.wait()
    half = HID // 2
    for r in range(RELS):
        h = lax.dot_general(
            adj_ref[r], grads_vmem[...], (((1,), (1,)), ((), ())), preferred_element_type=F32
        )
        out_ref[:, r * half : (r + 1) * half] = (h * (1.0 / FANOUT)).astype(BF16)


def hidden_half(place, grads, adj):
    vmem = pl.BlockSpec(memory_space=pltpu.VMEM)
    return pl.pallas_call(
        hidden_kernel,
        out_shape=jax.ShapeDtypeStruct((OWN, HALF), BF16),
        in_specs=[pl.BlockSpec(memory_space=pltpu.SMEM)]
        + [pl.BlockSpec(memory_space=pl.ANY)] * 4
        + [vmem],
        out_specs=vmem,
        scratch_shapes=[pltpu.VMEM((HID // 2, TGT), BF16), pltpu.SemaphoreType.DMA((4,))],
        compiler_params=pltpu.CompilerParams(vmem_limit_bytes=10 << 20),
        cost_estimate=pl.CostEstimate(
            flops=1_000_000_000, bytes_accessed=4 << 20, transcendentals=0
        ),
        name="hidden_half",
    )(place, *grads, adj)


def weave(low, high, odd):
    lane = lax.broadcasted_iota(I32, low.shape, 1)
    if odd:
        return jnp.where(lane < LANES // 2, pltpu.roll(low, LANES // 2, 1), high)
    return jnp.where(lane < LANES // 2, low, pltpu.roll(high, LANES // 2, 1))


def source_kernel(place_ref, mine_ref, far_ref, weight_ref, out_ref, hidden):
    first = place_ref[1] == 0
    for i in range(HALF // LANES):
        cols = slice(i * LANES, (i + 1) * LANES)
        mine, far = mine_ref[:, cols].astype(F32), far_ref[:, cols].astype(F32)
        low, high = jnp.where(first, mine, far), jnp.where(first, far, mine)
        for odd in range(2):
            to = (2 * i + odd) * LANES
            hidden[:, to : to + LANES] = weave(low, high, odd).astype(BF16)
    out_ref[...] = lax.dot_general(
        hidden[...], weight_ref[...], (((1,), (1,)), ((), ())), preferred_element_type=F32
    ).astype(BF16)


def source_rows(place, mine, far, weight):
    vmem = pl.BlockSpec(memory_space=pltpu.VMEM)
    return pl.pallas_call(
        source_kernel,
        out_shape=jax.ShapeDtypeStruct((OWN, D_IN), BF16),
        in_specs=[pl.BlockSpec(memory_space=pltpu.SMEM)] + [vmem] * 3,
        out_specs=vmem,
        scratch_shapes=[pltpu.VMEM((OWN, COLS), BF16)],
        compiler_params=pltpu.CompilerParams(vmem_limit_bytes=16 << 20),
        cost_estimate=pl.CostEstimate(
            flops=1_000_000_000, bytes_accessed=6 << 20, transcendentals=0
        ),
        name="source_rows",
    )(place, mine, far, weight)


def product_kernel(place_ref, mine_ref, far_ref, got_mine_ref, got_far_ref, f0_ref, f1_ref, *out):
    out_ref, chunks = out
    core = place_ref[1]
    tiles = HALF // LANES
    wide = 2 * LANES
    for which, own_ref, got_ref in ((core, mine_ref, got_far_ref), (1 - core, far_ref, got_mine_ref)):
        for b in range(HALF // wide):
            cols = slice(b * wide, (b + 1) * wide)
            p = jnp.dot(f0_ref[...], own_ref[:, cols], preferred_element_type=F32)
            p += jnp.dot(f1_ref[...], got_ref[:, cols], preferred_element_type=F32)
            for r in range(ROWS_OUT):
                for c in range(2):
                    at = r * 2 * tiles + which * tiles + 2 * b + c
                    part = p[r * PEERS : (r + 1) * PEERS, c * LANES : (c + 1) * LANES]
                    chunks[:, pl.ds(at, 1), :] = part[:, None, :]
    out_ref[...] = chunks[...].astype(BF16)


def products(place, mine, far, got_mine, got_far, f0, f1):
    vmem = pl.BlockSpec(memory_space=pltpu.VMEM)
    return pl.pallas_call(
        product_kernel,
        out_shape=jax.ShapeDtypeStruct((PEERS, CHUNK, LANES), BF16),
        in_specs=[pl.BlockSpec(memory_space=pltpu.SMEM)] + [vmem] * 6,
        out_specs=vmem,
        scratch_shapes=[pltpu.VMEM((PEERS, CHUNK, LANES), F32)],
        compiler_params=pltpu.CompilerParams(vmem_limit_bytes=20 << 20),
        cost_estimate=pl.CostEstimate(
            flops=1_000_000_000, bytes_accessed=5 << 20, transcendentals=0
        ),
        name="products",
    )(place, mine, far, got_mine, got_far, f0, f1)


def sum_kernel(scale, got_ref, out_ref, sums):
    total = got_ref[0].astype(F32)
    for d in range(1, PEERS):
        total += got_ref[d].astype(F32)
    sums[...] = total * scale
    tiles = HALF // LANES
    for r in range(ROWS_OUT):
        at = r * 2 * tiles
        low, high = sums[at : at + tiles, :], sums[at + tiles : at + 2 * tiles, :]
        for odd in range(2):
            both = weave(low, high, odd)
            for i in range(tiles):
                to = (2 * i + odd) * LANES
                out_ref[r : r + 1, to : to + LANES] = both[i : i + 1, :]


def sum_chunks(got, scale):
    vmem = pl.BlockSpec(memory_space=pltpu.VMEM)
    return pl.pallas_call(
        functools.partial(sum_kernel, scale),
        out_shape=jax.ShapeDtypeStruct((ROWS_OUT, COLS), F32),
        in_specs=[vmem],
        out_specs=vmem,
        scratch_shapes=[pltpu.VMEM((CHUNK, LANES), F32)],
        compiler_params=pltpu.CompilerParams(vmem_limit_bytes=14 << 20),
        cost_estimate=pl.CostEstimate(flops=1 << 20, bytes_accessed=2 << 20, transcendentals=0),
        name="sum_chunks",
    )(got)


def on_device(grad_out, src_feat, weight, nbr_slot, src_ids, valid_rows, block_rel):
    rel = lax.axis_index("rel")
    core = rel & 1
    place = jnp.stack([rel, core]).astype(I32)

    def along_z(v, k):
        return lax.ppermute(v, "rel", [(i, (i + 2 * k) % 8) for i in range(8)])

    def other_core(v):
        return lax.ppermute(v, "rel", [(i, i ^ 1) for i in range(8)])

    codes, own_grads = edge_codes(
        valid_rows, block_rel, src_ids[0], nbr_slot.transpose(1, 2, 0), grad_out.T
    )
    far = {k: along_z(codes, k) for k in (1, 3, 2)}
    grads = [along_z(own_grads, k) for k in (1, 2, 3)]
    planes = count_first(place, codes)
    planes = count_edges(place, [other_core(codes), far[1], far[3]], planes)
    planes = count_edges(place, [other_core(far[1]), other_core(far[3])], planes)
    last, grads[0], grads[2] = after([far[2], grads[0], grads[2]], planes)
    planes = count_edges(place, [last], planes)
    adj = count_last(place, other_core(last), planes)
    grads = [own_grads] + list(after(grads, adj))
    mine = hidden_half(place, grads, adj)
    other = hidden_half(place, [other_core(v) for v in grads], adj)

    old = jnp.arange(D_IN, dtype=I32)[:, None]
    new = jnp.arange(D_IN // 2, dtype=I32)[None, :]

    def half_feats(which):
        device = (new % PEERS) * 2 + which
        order = (old == device * ROWS_OUT + new // PEERS).astype(BF16)
        return lax.dot_general(
            order, src_feat, (((0,), (1,)), ((), ())), preferred_element_type=F32
        ).astype(BF16)

    feats = half_feats(core)
    feats_other = other_core(half_feats(1 - core))

    got_mine, got_other = other_core(mine), other_core(other)
    source_grad = source_rows(place, mine, other, weight)
    chunks = products(place, mine, other, got_mine, got_other, feats, feats_other)
    groups = [[2 * i + c for i in range(PEERS)] for c in range(2)]
    chunks = lax.all_to_all(
        chunks, ("dp", "rel"), 0, 0, tiled=True, axis_index_groups=groups
    )
    return source_grad, sum_chunks(chunks, float(TGT * 16) ** (-0.5))


def solution(mesh):
    return jax.shard_map(
        on_device,
        mesh=mesh,
        in_specs=(
            P("dp", "rel"),
            P(("dp", "rel"), None),
            P(),
            P("dp", "rel", None),
            P("dp", "rel", None),
            P("dp", "rel"),
            P("rel"),
        ),
        out_specs=(P(("dp", "rel"), None), P(("dp", "rel"), None)),
        check_vma=False,
    )
```

```python
import functools

import jax
import jax.numpy as jnp
from jax import lax
from jax.experimental import pallas as pl
from jax.experimental.pallas import tpu as pltpu
from jax.sharding import PartitionSpec as P

I32 = jnp.int32
BF16 = jnp.bfloat16
F32 = jnp.float32
D_IN = 768
HID = 512
RELS = 5
COLS = RELS * HID
FANOUT = 16
SLOTS = 512
TGT = 1024
BLKS = 8
POOL = 2048
OWN = 256
NO_EDGE = RELS * POOL
PLANES = 10
ROWS_OUT = 6
LANES = 128
CHUNK = 120
PEERS = 64
TILES = TGT // LANES
STEP = 2
PIECE = HID // 8


def edge_kernel(valid_ref, rel_ref, ids_ref, nbr_ref, out_ref):
    lane = lax.broadcasted_iota(I32, (8, LANES), 1)
    sub = lax.broadcasted_iota(I32, (8, LANES), 0)
    meta = jnp.zeros((8, LANES), I32)
    for b in range(BLKS):
        rel = rel_ref[b]
        limit = valid_ref[0, b]
        meta = jnp.where((sub == b) & (lane == 0), rel, meta)
        meta = jnp.where((sub == b) & (lane == 1), (limit + (STEP * LANES - 1)) // (STEP * LANES), meta)
        node = ids_ref[b : b + 1, :]
        code = rel * POOL + (node & 1792) + ((node & 7) << 5) + ((node >> 3) & 31)
        tables = [
            jnp.broadcast_to(code[:, i * LANES : (i + 1) * LANES], (8, LANES))
            for i in range(SLOTS // LANES)
        ]
        for t in range(TGT // LANES):
            cols = slice(t * LANES, (t + 1) * LANES)
            live = (lane + t * LANES) < limit
            halves = []
            for half in range(2):
                slot = nbr_ref[b, half * 8 : (half + 1) * 8, cols]
                low = slot & (LANES - 1)
                high = slot >> 7
                got = [
                    jnp.take_along_axis(table, low, axis=1, mode="promise_in_bounds")
                    for table in tables
                ]
                found = jnp.where(
                    high < 2,
                    jnp.where(high == 0, got[0], got[1]),
                    jnp.where(high == 2, got[2], got[3]),
                )
                halves.append(jnp.where(live, found, NO_EDGE))
            out_ref[b * TILES + t] = halves[0] | (halves[1] << 16)
    out_ref[BLKS * TILES] = meta


def edge_codes(valid_rows, block_rel, ids, nbr):
    return pl.pallas_call(
        edge_kernel,
        out_shape=jax.ShapeDtypeStruct((BLKS * TILES + 1, 8, LANES), I32),
        in_specs=[pl.BlockSpec(memory_space=pltpu.SMEM)] * 2
        + [pl.BlockSpec(memory_space=pltpu.VMEM)] * 2,
        out_specs=pl.BlockSpec(memory_space=pltpu.VMEM),
        cost_estimate=pl.CostEstimate(flops=0, bytes_accessed=1 << 20, transcendentals=0),
        name="edge_codes",
    )(valid_rows, block_rel, ids, nbr)


def full_add(a, b, c):
    x = a ^ b
    return x ^ c, (a & b) | (c & x)


def count_bits(masks, planes):
    carried = masks
    out = []
    for i in range(PLANES):
        cur = carried + [planes[i]]
        carried = []
        while len(cur) >= 3:
            s, c = full_add(cur[0], cur[1], cur[2])
            cur = cur[3:] + [s]
            carried.append(c)
        if len(cur) == 2:
            carried.append(cur[0] & cur[1])
            cur = [cur[0] ^ cur[1]]
        out.append(cur[0])
    return out


def swap_bits(a, b, shift, mask):
    if a is None and b is None:
        return a, b
    if b is None:
        t = lax.shift_right_logical(a, jnp.int32(shift)) & mask
        return a & mask, t
    t = (lax.shift_right_logical(a, jnp.int32(shift)) ^ b) & mask
    return a ^ (t << shift), b ^ t


def plane_bytes(planes):
    x = list(planes)
    for shift, mask in ((4, 0x0F0F0F0F), (2, 0x33333333), (1, 0x55555555)):
        for i in range(8):
            if not i & shift:
                x[i], x[i + shift] = swap_bits(x[i], x[i + shift], shift, mask)
    return x


def counts(planes):
    low = plane_bytes(planes[:8])
    high = plane_bytes(planes[8:] + [None] * (16 - PLANES))
    pair = 0x00FF00FF
    rows = [None] * 32
    for off in range(8):
        even = (low[off] & pair) | ((high[off] & pair) << 8)
        odd = (lax.shift_right_logical(low[off], jnp.int32(8)) & pair) | (high[off] & ~pair)
        for q, word in enumerate((even, odd)):
            rows[off + 8 * q] = (word & 0xFFFF).astype(F32)
            rows[off + 8 * q + 16] = lax.shift_right_logical(word, jnp.int32(16)).astype(F32)
    return jnp.concatenate(rows, axis=0).astype(BF16)


def start_loads(edges, words, meta, word_sems, meta_sems):
    loads = []
    for i, edge in enumerate(edges):
        m = pltpu.make_async_copy(edge.at[BLKS * TILES], meta.at[i], meta_sems.at[i])
        w = pltpu.make_async_copy(edge.at[pl.ds(0, BLKS * TILES)], words.at[i], word_sems.at[i])
        m.start()
        w.start()
        loads.append((m, w))
    return loads


def count_all(mine, loads, words, meta, keys, planes_ref):
    row = lax.broadcasted_iota(I32, (STEP, 8, LANES), 1)
    for i, load in enumerate(loads):
        for copy in load:
            copy.wait()

        def one_block(b, carry, i=i):
            rel = meta[i, b, 0]
            steps = meta[i, b, 1]
            word = words[i, pl.ds(b * TILES, TILES)]
            for half, code in enumerate((word & 0xFFFF, word >> 16)):
                keys[half, 0] = code >> 5
                keys[half, 1] = jnp.left_shift(jnp.int32(1), code & 31)
            target = row + (rel * (POOL // 32) + mine * (OWN // 32))

            def one_step(t, carry):
                at = pl.ds(t * STEP, STEP)
                masks = []
                for half in range(2):
                    for s in range(8):
                        key = jnp.broadcast_to(keys[half, 0, at, s : s + 1, :], target.shape)
                        bit = jnp.broadcast_to(keys[half, 1, at, s : s + 1, :], target.shape)
                        masks.append(jnp.where(key == target, bit, 0))
                new = count_bits(masks, [planes_ref[rel, p, at] for p in range(PLANES)])
                for p in range(PLANES):
                    planes_ref[rel, p, at] = new[p]
                return carry

            return lax.fori_loop(0, steps, one_step, carry)

        lax.fori_loop(0, BLKS, one_block, 0)


PLANE_SHAPE = (RELS, PLANES, TILES, 8, LANES)


def count_scratch(n):
    return [
        pltpu.VMEM((n, BLKS * TILES, 8, LANES), I32),
        pltpu.VMEM((2, 2, TILES, 8, LANES), I32),
        pltpu.SMEM((n, 8, LANES), I32),
        pltpu.SemaphoreType.DMA((n,)),
        pltpu.SemaphoreType.DMA((n,)),
    ]


def count_kernel(n, place_ref, *refs):
    edges = refs[:n]
    planes_ref, words, keys, meta, word_sems, meta_sems = refs[n + 1 :]
    loads = start_loads(edges, words, meta, word_sems, meta_sems)
    planes_ref[...] = refs[n][...]
    count_all(place_ref[0], loads, words, meta, keys, planes_ref)


def first_kernel(n, place_ref, *refs):
    edges = refs[:n]
    planes_ref, words, keys, meta, word_sems, meta_sems = refs[n:]
    loads = start_loads(edges, words, meta, word_sems, meta_sems)
    planes_ref[...] = jnp.zeros_like(planes_ref)
    count_all(place_ref[0], loads, words, meta, keys, planes_ref)


def count_first(place, edges):
    n = len(edges)
    return pl.pallas_call(
        functools.partial(first_kernel, n),
        out_shape=jax.ShapeDtypeStruct(PLANE_SHAPE, I32),
        in_specs=[pl.BlockSpec(memory_space=pltpu.SMEM)]
        + [pl.BlockSpec(memory_space=pl.ANY)] * n,
        out_specs=pl.BlockSpec(memory_space=pltpu.VMEM),
        scratch_shapes=count_scratch(n),
        compiler_params=pltpu.CompilerParams(vmem_limit_bytes=14 << 20),
        cost_estimate=pl.CostEstimate(
            flops=2_000_000_000, bytes_accessed=1 << 20, transcendentals=0
        ),
        name="count_first",
    )(place, *edges)


def count_edges(place, edges, planes):
    n = len(edges)
    vmem = pl.BlockSpec(memory_space=pltpu.VMEM)
    return pl.pallas_call(
        functools.partial(count_kernel, n),
        out_shape=jax.ShapeDtypeStruct(PLANE_SHAPE, I32),
        in_specs=[pl.BlockSpec(memory_space=pltpu.SMEM)]
        + [pl.BlockSpec(memory_space=pl.ANY)] * n
        + [vmem],
        out_specs=vmem,
        scratch_shapes=count_scratch(n),
        compiler_params=pltpu.CompilerParams(vmem_limit_bytes=14 << 20),
        cost_estimate=pl.CostEstimate(
            flops=n * 1_500_000_000, bytes_accessed=n << 19, transcendentals=0
        ),
        name="count_edges",
    )(place, *edges, planes)


def last_kernel(n, place_ref, *refs):
    edges = refs[:n]
    start_ref, adj_ref, words, keys, meta, word_sems, meta_sems, planes_ref = refs[n:]
    loads = start_loads(edges, words, meta, word_sems, meta_sems)
    planes_ref[...] = start_ref[...]
    count_all(place_ref[0], loads, words, meta, keys, planes_ref)
    for r in range(RELS):
        for t in range(TILES):
            adj_ref[r * OWN : (r + 1) * OWN, t * LANES : (t + 1) * LANES] = counts(
                [planes_ref[r, p, t] for p in range(PLANES)]
            )


def count_last(place, edges, planes):
    n = len(edges)
    vmem = pl.BlockSpec(memory_space=pltpu.VMEM)
    return pl.pallas_call(
        functools.partial(last_kernel, n),
        out_shape=jax.ShapeDtypeStruct((RELS * OWN, TGT), BF16),
        in_specs=[pl.BlockSpec(memory_space=pltpu.SMEM)]
        + [pl.BlockSpec(memory_space=pl.ANY)] * n
        + [vmem],
        out_specs=vmem,
        scratch_shapes=count_scratch(n) + [pltpu.VMEM(PLANE_SHAPE, I32)],
        compiler_params=pltpu.CompilerParams(vmem_limit_bytes=14 << 20),
        cost_estimate=pl.CostEstimate(
            flops=6_000_000_000, bytes_accessed=4 << 20, transcendentals=0
        ),
        name="count_last",
    )(place, *edges, planes)


def hidden_kernel(place_ref, *refs):
    grads = refs[:8]
    adj_ref, out_ref, grads_vmem, sems = refs[8:]
    copies = []
    for i in range(8):
        z = (place_ref[0] // 2 - i % 4) & 3
        core = place_ref[1] if i < 4 else 1 - place_ref[1]
        rows = pl.ds(pl.multiple_of((z * 2 + core) * PIECE, PIECE), PIECE)
        copies.append(pltpu.make_async_copy(grads[i], grads_vmem.at[rows], sems.at[i]))
        copies[i].start()
    for copy in copies:
        copy.wait()
    wide = 2 * LANES
    for b in range(HID // wide):
        h = lax.dot_general(
            adj_ref[...],
            grads_vmem[b * wide : (b + 1) * wide, :],
            (((1,), (1,)), ((), ())),
            preferred_element_type=F32,
        )
        h = (h * (1.0 / FANOUT)).astype(BF16)
        for r in range(RELS):
            to = r * HID + b * wide
            out_ref[:, to : to + wide] = h[r * OWN : (r + 1) * OWN, :]


def hidden_rows(place, grads, adj):
    vmem = pl.BlockSpec(memory_space=pltpu.VMEM)
    return pl.pallas_call(
        hidden_kernel,
        out_shape=jax.ShapeDtypeStruct((OWN, COLS), BF16),
        in_specs=[pl.BlockSpec(memory_space=pltpu.SMEM)]
        + [pl.BlockSpec(memory_space=pl.ANY)] * 8
        + [vmem],
        out_specs=vmem,
        scratch_shapes=[pltpu.VMEM((HID, TGT), BF16), pltpu.SemaphoreType.DMA((8,))],
        compiler_params=pltpu.CompilerParams(vmem_limit_bytes=14 << 20),
        cost_estimate=pl.CostEstimate(
            flops=2_000_000_000, bytes_accessed=4 << 20, transcendentals=0
        ),
        name="hidden_rows",
    )(place, *grads, adj)


def source_kernel(hidden_ref, weight_ref, out_ref):
    out_ref[...] = lax.dot_general(
        hidden_ref[...], weight_ref[...], (((1,), (1,)), ((), ())), preferred_element_type=F32
    ).astype(BF16)


def source_rows(hidden, weight):
    vmem = pl.BlockSpec(memory_space=pltpu.VMEM)
    return pl.pallas_call(
        source_kernel,
        out_shape=jax.ShapeDtypeStruct((OWN, D_IN), BF16),
        in_specs=[vmem] * 2,
        out_specs=vmem,
        compiler_params=pltpu.CompilerParams(vmem_limit_bytes=16 << 20),
        cost_estimate=pl.CostEstimate(
            flops=1_000_000_000, bytes_accessed=6 << 20, transcendentals=0
        ),
        name="source_rows",
    )(hidden, weight)


def chunk_row(r, tile):
    return tile // 4 * 24 + tile // 2 % 2 * 12 + r * 2 + tile % 2


def product_kernel(h0_ref, h1_ref, f0_ref, f1_ref, out_ref, chunks):
    wide = 2 * LANES
    for pair in range(COLS // (2 * wide)):
        parts = []
        for b in (2 * pair, 2 * pair + 1):
            cols = slice(b * wide, (b + 1) * wide)
            p = jnp.dot(f0_ref[...], h0_ref[:, cols], preferred_element_type=F32)
            p += jnp.dot(f1_ref[...], h1_ref[:, cols], preferred_element_type=F32)
            for r in range(ROWS_OUT):
                rows = p[r * PEERS : (r + 1) * PEERS]
                parts += [rows[:, c * LANES : (c + 1) * LANES] for c in range(2)]
        for g in range(3):
            at = pair * 24 + g * 8
            for d in range(0, PEERS, 8):
                block = jnp.stack([part[d : d + 8] for part in parts[g * 8 : (g + 1) * 8]], axis=0)
                chunks[d : d + 8, at : at + 8, :] = jnp.swapaxes(block, 0, 1)
    out_ref[...] = chunks[...].astype(BF16)


def products(h0, h1, f0, f1):
    vmem = pl.BlockSpec(memory_space=pltpu.VMEM)
    return pl.pallas_call(
        product_kernel,
        out_shape=jax.ShapeDtypeStruct((PEERS, CHUNK, LANES), BF16),
        in_specs=[vmem] * 4,
        out_specs=vmem,
        scratch_shapes=[pltpu.VMEM((PEERS, CHUNK, LANES), F32)],
        compiler_params=pltpu.CompilerParams(vmem_limit_bytes=20 << 20),
        cost_estimate=pl.CostEstimate(
            flops=1_000_000_000, bytes_accessed=5 << 20, transcendentals=0
        ),
        name="products",
    )(h0, h1, f0, f1)


def sum_kernel(scale, got_ref, out_ref, sums):
    tiles = COLS // LANES
    total = got_ref[0].astype(F32)
    for d in range(1, PEERS):
        total += got_ref[d].astype(F32)
    sums[...] = total * scale
    for r in range(ROWS_OUT):
        for i in range(tiles):
            at = chunk_row(r, i)
            out_ref[r : r + 1, i * LANES : (i + 1) * LANES] = sums[at : at + 1, :]


def sum_chunks(got, scale):
    vmem = pl.BlockSpec(memory_space=pltpu.VMEM)
    return pl.pallas_call(
        functools.partial(sum_kernel, scale),
        out_shape=jax.ShapeDtypeStruct((ROWS_OUT, COLS), F32),
        in_specs=[vmem],
        out_specs=vmem,
        scratch_shapes=[pltpu.VMEM((CHUNK, LANES), F32)],
        compiler_params=pltpu.CompilerParams(vmem_limit_bytes=14 << 20),
        cost_estimate=pl.CostEstimate(flops=1 << 20, bytes_accessed=2 << 20, transcendentals=0),
        name="sum_chunks",
    )(got)


def on_device(grad_out, src_feat, weight, nbr_slot, src_ids, valid_rows, block_rel):
    rel = lax.axis_index("rel")
    core = rel & 1
    place = jnp.stack([rel, core]).astype(I32)

    def along_z(v, k):
        return lax.ppermute(v, "rel", [(i, (i + 2 * k) % 8) for i in range(8)])

    def other_core(v):
        return lax.ppermute(v, "rel", [(i, i ^ 1) for i in range(8)])

    codes = edge_codes(valid_rows, block_rel, src_ids[0], nbr_slot.transpose(1, 2, 0))
    far = {k: along_z(codes, k) for k in (1, 3, 2)}
    grads = {0: grad_out.T}
    for k in (1, 3, 2):
        grads[k] = along_z(grads[0], k)
    pieces = [grads[k] for k in range(4)]
    pieces += [other_core(v) for v in pieces]
    planes = count_first(place, [codes, other_core(codes)])
    planes = count_edges(place, [far[k] for k in (1, 3, 2)], planes)
    adj = count_last(place, [other_core(far[k]) for k in (1, 3, 2)], planes)

    old = jnp.arange(D_IN, dtype=I32)[:, None]
    new = jnp.arange(D_IN // 2, dtype=I32)[None, :]

    def half_feats(which):
        device = (new % PEERS) * 2 + which
        order = (old == device * ROWS_OUT + new // PEERS).astype(BF16)
        return lax.dot_general(
            order, src_feat, (((0,), (1,)), ((), ())), preferred_element_type=F32
        ).astype(BF16)

    feats = half_feats(core)
    feats_other = other_core(half_feats(1 - core))

    hidden = hidden_rows(place, pieces, adj)
    got = other_core(hidden)
    source_grad = source_rows(hidden, weight)
    chunks = products(hidden, got, feats, feats_other)
    groups = [[2 * i + c for i in range(PEERS)] for c in range(2)]
    chunks = lax.all_to_all(
        chunks, ("dp", "rel"), 0, 0, tiled=True, axis_index_groups=groups
    )
    return source_grad, sum_chunks(chunks, float(TGT * 16) ** (-0.5))


def solution(mesh):
    return jax.shard_map(
        on_device,
        mesh=mesh,
        in_specs=(
            P("dp", "rel"),
            P(("dp", "rel"), None),
            P(),
            P("dp", "rel", None),
            P("dp", "rel", None),
            P("dp", "rel"),
            P("rel"),
        ),
        out_specs=(P(("dp", "rel"), None), P(("dp", "rel"), None)),
        check_vma=False,
    )
```

```python
import functools

import jax
import jax.numpy as jnp
from jax import lax
from jax.experimental import pallas as pl
from jax.experimental.pallas import tpu as pltpu
from jax.sharding import PartitionSpec as P

I32 = jnp.int32
BF16 = jnp.bfloat16
F32 = jnp.float32
D_IN = 768
HID = 512
RELS = 5
COLS = RELS * HID
FANOUT = 16
SLOTS = 512
TGT = 1024
BLKS = 8
POOL = 2048
OWN = 256
NO_EDGE = RELS * POOL
PLANES = 10
ROWS_OUT = 6
LANES = 128
CHUNK = 120
PEERS = 64
TILES = TGT // LANES
STEP = 2
PIECE = HID // 8


def edge_kernel(valid_ref, rel_ref, ids_ref, nbr_ref, out_ref):
    lane = lax.broadcasted_iota(I32, (8, LANES), 1)
    sub = lax.broadcasted_iota(I32, (8, LANES), 0)
    meta = jnp.zeros((8, LANES), I32)
    for b in range(BLKS):
        rel = rel_ref[b]
        limit = valid_ref[0, b]
        meta = jnp.where((sub == b) & (lane == 0), rel, meta)
        meta = jnp.where((sub == b) & (lane == 1), (limit + (STEP * LANES - 1)) // (STEP * LANES), meta)
        node = ids_ref[b : b + 1, :]
        code = rel * POOL + (node & 1792) + ((node & 7) << 5) + ((node >> 3) & 31)
        tables = [
            jnp.broadcast_to(code[:, i * LANES : (i + 1) * LANES], (8, LANES))
            for i in range(SLOTS // LANES)
        ]
        for t in range(TGT // LANES):
            cols = slice(t * LANES, (t + 1) * LANES)
            live = (lane + t * LANES) < limit
            halves = []
            for half in range(2):
                slot = nbr_ref[b, half * 8 : (half + 1) * 8, cols]
                low = slot & (LANES - 1)
                high = slot >> 7
                got = [
                    jnp.take_along_axis(table, low, axis=1, mode="promise_in_bounds")
                    for table in tables
                ]
                found = jnp.where(
                    high < 2,
                    jnp.where(high == 0, got[0], got[1]),
                    jnp.where(high == 2, got[2], got[3]),
                )
                halves.append(jnp.where(live, found, NO_EDGE))
            out_ref[b * TILES + t] = halves[0] | (halves[1] << 16)
    out_ref[BLKS * TILES] = meta


def edge_codes(valid_rows, block_rel, ids, nbr):
    return pl.pallas_call(
        edge_kernel,
        out_shape=jax.ShapeDtypeStruct((BLKS * TILES + 1, 8, LANES), I32),
        in_specs=[pl.BlockSpec(memory_space=pltpu.SMEM)] * 2
        + [pl.BlockSpec(memory_space=pltpu.VMEM)] * 2,
        out_specs=pl.BlockSpec(memory_space=pltpu.VMEM),
        cost_estimate=pl.CostEstimate(flops=0, bytes_accessed=1 << 20, transcendentals=0),
        name="edge_codes",
    )(valid_rows, block_rel, ids, nbr)


def full_add(a, b, c):
    x = a ^ b
    return x ^ c, (a & b) | (c & x)


def count_bits(masks, planes):
    carried = masks
    out = []
    for i in range(PLANES):
        cur = carried + [planes[i]]
        carried = []
        while len(cur) >= 3:
            s, c = full_add(cur[0], cur[1], cur[2])
            cur = cur[3:] + [s]
            carried.append(c)
        if len(cur) == 2:
            carried.append(cur[0] & cur[1])
            cur = [cur[0] ^ cur[1]]
        out.append(cur[0])
    return out


def swap_bits(a, b, shift, mask):
    if a is None and b is None:
        return a, b
    if b is None:
        t = lax.shift_right_logical(a, jnp.int32(shift)) & mask
        return a & mask, t
    t = (lax.shift_right_logical(a, jnp.int32(shift)) ^ b) & mask
    return a ^ (t << shift), b ^ t


def plane_bytes(planes):
    x = list(planes)
    for shift, mask in ((4, 0x0F0F0F0F), (2, 0x33333333), (1, 0x55555555)):
        for i in range(8):
            if not i & shift:
                x[i], x[i + shift] = swap_bits(x[i], x[i + shift], shift, mask)
    return x


def counts(planes):
    low = plane_bytes(planes[:8])
    high = plane_bytes(planes[8:] + [None] * (16 - PLANES))
    pair = 0x00FF00FF
    rows = [None] * 32
    for off in range(8):
        even = (low[off] & pair) | ((high[off] & pair) << 8)
        odd = (lax.shift_right_logical(low[off], jnp.int32(8)) & pair) | (high[off] & ~pair)
        for q, word in enumerate((even, odd)):
            rows[off + 8 * q] = (word & 0xFFFF).astype(F32)
            rows[off + 8 * q + 16] = lax.shift_right_logical(word, jnp.int32(16)).astype(F32)
    return jnp.concatenate(rows, axis=0).astype(BF16)


def start_loads(edges, words, meta, word_sems, meta_sems):
    loads = []
    for i, edge in enumerate(edges):
        m = pltpu.make_async_copy(edge.at[BLKS * TILES], meta.at[i], meta_sems.at[i])
        w = pltpu.make_async_copy(edge.at[pl.ds(0, BLKS * TILES)], words.at[i], word_sems.at[i])
        m.start()
        w.start()
        loads.append((m, w))
    return loads


def count_all(mine, loads, words, meta, keys, planes_ref):
    row = lax.broadcasted_iota(I32, (STEP, 8, LANES), 1)
    for i, load in enumerate(loads):
        for copy in load:
            copy.wait()

        def one_block(b, carry, i=i):
            rel = meta[i, b, 0]
            steps = meta[i, b, 1]
            word = words[i, pl.ds(b * TILES, TILES)]
            for half, code in enumerate((word & 0xFFFF, word >> 16)):
                keys[half, 0] = code >> 5
                keys[half, 1] = jnp.left_shift(jnp.int32(1), code & 31)
            target = row + (rel * (POOL // 32) + mine * (OWN // 32))

            def one_step(t, carry):
                at = pl.ds(t * STEP, STEP)
                masks = []
                for half in range(2):
                    for s in range(8):
                        key = jnp.broadcast_to(keys[half, 0, at, s : s + 1, :], target.shape)
                        bit = jnp.broadcast_to(keys[half, 1, at, s : s + 1, :], target.shape)
                        masks.append(jnp.where(key == target, bit, 0))
                new = count_bits(masks, [planes_ref[rel, p, at] for p in range(PLANES)])
                for p in range(PLANES):
                    planes_ref[rel, p, at] = new[p]
                return carry

            return lax.fori_loop(0, steps, one_step, carry)

        lax.fori_loop(0, BLKS, one_block, 0)


PLANE_SHAPE = (RELS, PLANES, TILES, 8, LANES)


def count_scratch(n):
    return [
        pltpu.VMEM((n, BLKS * TILES, 8, LANES), I32),
        pltpu.VMEM((2, 2, TILES, 8, LANES), I32),
        pltpu.SMEM((n, 8, LANES), I32),
        pltpu.SemaphoreType.DMA((n,)),
        pltpu.SemaphoreType.DMA((n,)),
    ]


def count_kernel(n, place_ref, *refs):
    edges = refs[:n]
    planes_ref, words, keys, meta, word_sems, meta_sems = refs[n + 1 :]
    loads = start_loads(edges, words, meta, word_sems, meta_sems)
    planes_ref[...] = refs[n][...]
    count_all(place_ref[0], loads, words, meta, keys, planes_ref)


def first_kernel(n, place_ref, *refs):
    edges = refs[:n]
    planes_ref, words, keys, meta, word_sems, meta_sems = refs[n:]
    loads = start_loads(edges, words, meta, word_sems, meta_sems)
    planes_ref[...] = jnp.zeros_like(planes_ref)
    count_all(place_ref[0], loads, words, meta, keys, planes_ref)


def count_first(place, edges):
    n = len(edges)
    return pl.pallas_call(
        functools.partial(first_kernel, n),
        out_shape=jax.ShapeDtypeStruct(PLANE_SHAPE, I32),
        in_specs=[pl.BlockSpec(memory_space=pltpu.SMEM)]
        + [pl.BlockSpec(memory_space=pl.ANY)] * n,
        out_specs=pl.BlockSpec(memory_space=pltpu.VMEM),
        scratch_shapes=count_scratch(n),
        compiler_params=pltpu.CompilerParams(vmem_limit_bytes=14 << 20),
        cost_estimate=pl.CostEstimate(
            flops=2_000_000_000, bytes_accessed=1 << 20, transcendentals=0
        ),
        name="count_first",
    )(place, *edges)


def count_edges(place, edges, planes):
    n = len(edges)
    vmem = pl.BlockSpec(memory_space=pltpu.VMEM)
    return pl.pallas_call(
        functools.partial(count_kernel, n),
        out_shape=jax.ShapeDtypeStruct(PLANE_SHAPE, I32),
        in_specs=[pl.BlockSpec(memory_space=pltpu.SMEM)]
        + [pl.BlockSpec(memory_space=pl.ANY)] * n
        + [vmem],
        out_specs=vmem,
        scratch_shapes=count_scratch(n),
        compiler_params=pltpu.CompilerParams(vmem_limit_bytes=14 << 20),
        cost_estimate=pl.CostEstimate(
            flops=n * 1_500_000_000, bytes_accessed=n << 19, transcendentals=0
        ),
        name="count_edges",
    )(place, *edges, planes)


def hidden_kernel(n, place_ref, *refs):
    edges, pieces = refs[:n], refs[n : n + 8]
    start_ref, out_ref, words, keys, meta, word_sems, meta_sems = refs[n + 8 : n + 15]
    planes_ref, adj, grads_vmem, sems = refs[n + 15 :]
    loads = start_loads(edges, words, meta, word_sems, meta_sems)
    copies = []
    for i in range(8):
        z = (place_ref[0] // 2 - i % 4) & 3
        core = place_ref[1] if i < 4 else 1 - place_ref[1]
        rows = pl.ds(pl.multiple_of((z * 2 + core) * PIECE, PIECE), PIECE)
        copies.append(pltpu.make_async_copy(pieces[i], grads_vmem.at[rows], sems.at[i]))
        copies[i].start()
    planes_ref[...] = start_ref[...]
    count_all(place_ref[0], loads, words, meta, keys, planes_ref)
    for r in range(RELS):
        for t in range(TILES):
            adj[r * OWN : (r + 1) * OWN, t * LANES : (t + 1) * LANES] = counts(
                [planes_ref[r, p, t] for p in range(PLANES)]
            )
    for copy in copies:
        copy.wait()
    wide = 2 * LANES
    for b in range(HID // wide):
        h = lax.dot_general(
            adj[...],
            grads_vmem[b * wide : (b + 1) * wide, :],
            (((1,), (1,)), ((), ())),
            preferred_element_type=F32,
        )
        h = (h * (1.0 / FANOUT)).astype(BF16)
        for r in range(RELS):
            to = r * HID + b * wide
            out_ref[:, to : to + wide] = h[r * OWN : (r + 1) * OWN, :]


def hidden_rows(place, edges, pieces, planes):
    n = len(edges)
    vmem = pl.BlockSpec(memory_space=pltpu.VMEM)
    return pl.pallas_call(
        functools.partial(hidden_kernel, n),
        out_shape=jax.ShapeDtypeStruct((OWN, COLS), BF16),
        in_specs=[pl.BlockSpec(memory_space=pltpu.SMEM)]
        + [pl.BlockSpec(memory_space=pl.ANY)] * (n + 8)
        + [vmem],
        out_specs=vmem,
        scratch_shapes=count_scratch(n)
        + [
            pltpu.VMEM(PLANE_SHAPE, I32),
            pltpu.VMEM((RELS * OWN, TGT), BF16),
            pltpu.VMEM((HID, TGT), BF16),
            pltpu.SemaphoreType.DMA((8,)),
        ],
        compiler_params=pltpu.CompilerParams(vmem_limit_bytes=20 << 20),
        cost_estimate=pl.CostEstimate(
            flops=6_000_000_000, bytes_accessed=4 << 20, transcendentals=0
        ),
        name="hidden_rows",
    )(place, *edges, *pieces, planes)


def after_kernel(*refs):
    pass


def after(values, earlier):
    n = len(values)
    anywhere = pl.BlockSpec(memory_space=pl.ANY)
    return pl.pallas_call(
        after_kernel,
        out_shape=[jax.ShapeDtypeStruct(v.shape, v.dtype) for v in values],
        in_specs=[anywhere] * (n + 1),
        out_specs=[anywhere] * n,
        input_output_aliases={i: i for i in range(n)},
        compiler_params=pltpu.CompilerParams(vmem_limit_bytes=1 << 20),
        cost_estimate=pl.CostEstimate(flops=1000, bytes_accessed=1 << 10, transcendentals=0),
        name="after",
    )(*values, earlier)


def source_kernel(hidden_ref, weight_ref, out_ref):
    out_ref[...] = lax.dot_general(
        hidden_ref[...], weight_ref[...], (((1,), (1,)), ((), ())), preferred_element_type=F32
    ).astype(BF16)


def source_rows(hidden, weight):
    vmem = pl.BlockSpec(memory_space=pltpu.VMEM)
    return pl.pallas_call(
        source_kernel,
        out_shape=jax.ShapeDtypeStruct((OWN, D_IN), BF16),
        in_specs=[vmem] * 2,
        out_specs=vmem,
        compiler_params=pltpu.CompilerParams(vmem_limit_bytes=16 << 20),
        cost_estimate=pl.CostEstimate(
            flops=1_000_000_000, bytes_accessed=6 << 20, transcendentals=0
        ),
        name="source_rows",
    )(hidden, weight)


def chunk_row(r, tile):
    return tile // 4 * 24 + tile // 2 % 2 * 12 + r * 2 + tile % 2


def product_kernel(h0_ref, h1_ref, f0_ref, f1_ref, out_ref, chunks):
    wide = 2 * LANES
    for pair in range(COLS // (2 * wide)):
        parts = []
        for b in (2 * pair, 2 * pair + 1):
            cols = slice(b * wide, (b + 1) * wide)
            p = jnp.dot(f0_ref[...], h0_ref[:, cols], preferred_element_type=F32)
            p += jnp.dot(f1_ref[...], h1_ref[:, cols], preferred_element_type=F32)
            for r in range(ROWS_OUT):
                rows = p[r * PEERS : (r + 1) * PEERS]
                parts += [rows[:, c * LANES : (c + 1) * LANES] for c in range(2)]
        for g in range(3):
            at = pair * 24 + g * 8
            for d in range(0, PEERS, 8):
                block = jnp.stack([part[d : d + 8] for part in parts[g * 8 : (g + 1) * 8]], axis=0)
                chunks[d : d + 8, at : at + 8, :] = jnp.swapaxes(block, 0, 1)
    out_ref[...] = chunks[...].astype(BF16)


def products(h0, h1, f0, f1):
    vmem = pl.BlockSpec(memory_space=pltpu.VMEM)
    return pl.pallas_call(
        product_kernel,
        out_shape=jax.ShapeDtypeStruct((PEERS, CHUNK, LANES), BF16),
        in_specs=[vmem] * 4,
        out_specs=vmem,
        scratch_shapes=[pltpu.VMEM((PEERS, CHUNK, LANES), F32)],
        compiler_params=pltpu.CompilerParams(vmem_limit_bytes=20 << 20),
        cost_estimate=pl.CostEstimate(
            flops=1_000_000_000, bytes_accessed=5 << 20, transcendentals=0
        ),
        name="products",
    )(h0, h1, f0, f1)


def sum_kernel(scale, got_ref, out_ref, sums):
    tiles = COLS // LANES
    total = got_ref[0].astype(F32)
    for d in range(1, PEERS):
        total += got_ref[d].astype(F32)
    sums[...] = total * scale
    for r in range(ROWS_OUT):
        for i in range(tiles):
            at = chunk_row(r, i)
            out_ref[r : r + 1, i * LANES : (i + 1) * LANES] = sums[at : at + 1, :]


def sum_chunks(got, scale):
    vmem = pl.BlockSpec(memory_space=pltpu.VMEM)
    return pl.pallas_call(
        functools.partial(sum_kernel, scale),
        out_shape=jax.ShapeDtypeStruct((ROWS_OUT, COLS), F32),
        in_specs=[vmem],
        out_specs=vmem,
        scratch_shapes=[pltpu.VMEM((CHUNK, LANES), F32)],
        compiler_params=pltpu.CompilerParams(vmem_limit_bytes=14 << 20),
        cost_estimate=pl.CostEstimate(flops=1 << 20, bytes_accessed=2 << 20, transcendentals=0),
        name="sum_chunks",
    )(got)


def on_device(grad_out, src_feat, weight, nbr_slot, src_ids, valid_rows, block_rel):
    rel = lax.axis_index("rel")
    core = rel & 1
    place = jnp.stack([rel, core]).astype(I32)

    def along_z(v, k):
        return lax.ppermute(v, "rel", [(i, (i + 2 * k) % 8) for i in range(8)])

    def other_core(v):
        return lax.ppermute(v, "rel", [(i, i ^ 1) for i in range(8)])

    codes = edge_codes(valid_rows, block_rel, src_ids[0], nbr_slot.transpose(1, 2, 0))
    far = {k: along_z(codes, k) for k in (1, 3)}
    own_grads = grad_out.T
    up, down = along_z(own_grads, 1), along_z(own_grads, 3)
    planes = count_first(place, [codes, other_core(codes)])
    far[1], down = after([far[1], down], planes)
    far[2], twice_down = along_z(far[1], 1), along_z(down, 3)
    planes = count_edges(place, [far[1], far[3]], planes)
    planes = count_edges(place, [other_core(far[1]), other_core(far[3])], planes)
    far[2], *pieces = after([far[2], up, twice_down, down], planes)
    pieces = [own_grads] + pieces
    pieces += [other_core(v) for v in pieces]

    old = jnp.arange(D_IN, dtype=I32)[:, None]
    new = jnp.arange(D_IN // 2, dtype=I32)[None, :]

    def half_feats(which):
        device = (new % PEERS) * 2 + which
        order = (old == device * ROWS_OUT + new // PEERS).astype(BF16)
        return lax.dot_general(
            order, src_feat, (((0,), (1,)), ((), ())), preferred_element_type=F32
        ).astype(BF16)

    feats = half_feats(core)
    feats_other = other_core(half_feats(1 - core))

    hidden = hidden_rows(place, [far[2], other_core(far[2])], pieces, planes)
    got = other_core(hidden)
    source_grad = source_rows(hidden, weight)
    chunks = products(hidden, got, feats, feats_other)
    groups = [[2 * i + c for i in range(PEERS)] for c in range(2)]
    chunks = lax.all_to_all(
        chunks, ("dp", "rel"), 0, 0, tiled=True, axis_index_groups=groups
    )
    return source_grad, sum_chunks(chunks, float(TGT * 16) ** (-0.5))


def solution(mesh):
    return jax.shard_map(
        on_device,
        mesh=mesh,
        in_specs=(
            P("dp", "rel"),
            P(("dp", "rel"), None),
            P(),
            P("dp", "rel", None),
            P("dp", "rel", None),
            P("dp", "rel"),
            P("rel"),
        ),
        out_specs=(P(("dp", "rel"), None), P(("dp", "rel"), None)),
        check_vma=False,
    )
```

```python
import functools

import jax
import jax.numpy as jnp
from jax import lax
from jax.experimental import pallas as pl
from jax.experimental.pallas import tpu as pltpu
from jax.sharding import PartitionSpec as P

I32 = jnp.int32
BF16 = jnp.bfloat16
F32 = jnp.float32
D_IN = 768
HID = 512
RELS = 5
COLS = RELS * HID
FANOUT = 16
SLOTS = 512
TGT = 1024
BLKS = 8
POOL = 2048
OWN = 256
NO_EDGE = RELS * POOL
PLANES = 10
ROWS_OUT = 6
LANES = 128
CHUNK = 120
PEERS = 64
TILES = TGT // LANES
STEP = 2
PIECE = HID // 8


def edge_kernel(valid_ref, rel_ref, ids_ref, nbr_ref, out_ref):
    lane = lax.broadcasted_iota(I32, (8, LANES), 1)
    sub = lax.broadcasted_iota(I32, (8, LANES), 0)
    meta = jnp.zeros((8, LANES), I32)
    for b in range(BLKS):
        rel = rel_ref[b]
        limit = valid_ref[0, b]
        meta = jnp.where((sub == b) & (lane == 0), rel, meta)
        meta = jnp.where((sub == b) & (lane == 1), (limit + (STEP * LANES - 1)) // (STEP * LANES), meta)
        node = ids_ref[b : b + 1, :]
        code = rel * POOL + (node & 1792) + ((node & 7) << 5) + ((node >> 3) & 31)
        tables = [
            jnp.broadcast_to(code[:, i * LANES : (i + 1) * LANES], (8, LANES))
            for i in range(SLOTS // LANES)
        ]
        for t in range(TGT // LANES):
            cols = slice(t * LANES, (t + 1) * LANES)
            live = (lane + t * LANES) < limit
            halves = []
            for half in range(2):
                slot = nbr_ref[b, half * 8 : (half + 1) * 8, cols]
                low = slot & (LANES - 1)
                high = slot >> 7
                got = [
                    jnp.take_along_axis(table, low, axis=1, mode="promise_in_bounds")
                    for table in tables
                ]
                found = jnp.where(
                    high < 2,
                    jnp.where(high == 0, got[0], got[1]),
                    jnp.where(high == 2, got[2], got[3]),
                )
                halves.append(jnp.where(live, found, NO_EDGE))
            out_ref[b * TILES + t] = halves[0] | (halves[1] << 16)
    out_ref[BLKS * TILES] = meta


def edge_codes(valid_rows, block_rel, ids, nbr):
    return pl.pallas_call(
        edge_kernel,
        out_shape=jax.ShapeDtypeStruct((BLKS * TILES + 1, 8, LANES), I32),
        in_specs=[pl.BlockSpec(memory_space=pltpu.SMEM)] * 2
        + [pl.BlockSpec(memory_space=pltpu.VMEM)] * 2,
        out_specs=pl.BlockSpec(memory_space=pltpu.VMEM),
        cost_estimate=pl.CostEstimate(flops=0, bytes_accessed=1 << 20, transcendentals=0),
        name="edge_codes",
    )(valid_rows, block_rel, ids, nbr)


def full_add(a, b, c):
    x = a ^ b
    return x ^ c, (a & b) | (c & x)


def count_bits(masks, planes):
    carried = masks
    out = []
    for i in range(PLANES):
        cur = carried + [planes[i]]
        carried = []
        while len(cur) >= 3:
            s, c = full_add(cur[0], cur[1], cur[2])
            cur = cur[3:] + [s]
            carried.append(c)
        if len(cur) == 2:
            carried.append(cur[0] & cur[1])
            cur = [cur[0] ^ cur[1]]
        out.append(cur[0])
    return out


def swap_bits(a, b, shift, mask):
    if a is None and b is None:
        return a, b
    if b is None:
        t = lax.shift_right_logical(a, jnp.int32(shift)) & mask
        return a & mask, t
    t = (lax.shift_right_logical(a, jnp.int32(shift)) ^ b) & mask
    return a ^ (t << shift), b ^ t


def plane_bytes(planes):
    x = list(planes)
    for shift, mask in ((4, 0x0F0F0F0F), (2, 0x33333333), (1, 0x55555555)):
        for i in range(8):
            if not i & shift:
                x[i], x[i + shift] = swap_bits(x[i], x[i + shift], shift, mask)
    return x


def counts(planes):
    low = plane_bytes(planes[:8])
    high = plane_bytes(planes[8:] + [None] * (16 - PLANES))
    pair = 0x00FF00FF
    rows = [None] * 32
    for off in range(8):
        even = (low[off] & pair) | ((high[off] & pair) << 8)
        odd = (lax.shift_right_logical(low[off], jnp.int32(8)) & pair) | (high[off] & ~pair)
        for q, word in enumerate((even, odd)):
            rows[off + 8 * q] = (word & 0xFFFF).astype(F32)
            rows[off + 8 * q + 16] = lax.shift_right_logical(word, jnp.int32(16)).astype(F32)
    return jnp.concatenate(rows, axis=0).astype(BF16)


def start_loads(edges, words, meta, word_sems, meta_sems):
    loads = []
    for i, edge in enumerate(edges):
        m = pltpu.make_async_copy(edge.at[BLKS * TILES], meta.at[i], meta_sems.at[i])
        w = pltpu.make_async_copy(edge.at[pl.ds(0, BLKS * TILES)], words.at[i], word_sems.at[i])
        m.start()
        w.start()
        loads.append((m, w))
    return loads


def count_all(mine, loads, words, meta, keys, planes_ref):
    row = lax.broadcasted_iota(I32, (STEP, 8, LANES), 1)
    for i, load in enumerate(loads):
        for copy in load:
            copy.wait()

        def one_block(b, carry, i=i):
            rel = meta[i, b, 0]
            steps = meta[i, b, 1]
            word = words[i, pl.ds(b * TILES, TILES)]
            for half, code in enumerate((word & 0xFFFF, word >> 16)):
                keys[half, 0] = code >> 5
                keys[half, 1] = jnp.left_shift(jnp.int32(1), code & 31)
            target = row + (rel * (POOL // 32) + mine * (OWN // 32))

            def one_step(t, carry):
                at = pl.ds(t * STEP, STEP)
                masks = []
                for half in range(2):
                    for s in range(8):
                        key = jnp.broadcast_to(keys[half, 0, at, s : s + 1, :], target.shape)
                        bit = jnp.broadcast_to(keys[half, 1, at, s : s + 1, :], target.shape)
                        masks.append(jnp.where(key == target, bit, 0))
                new = count_bits(masks, [planes_ref[rel, p, at] for p in range(PLANES)])
                for p in range(PLANES):
                    planes_ref[rel, p, at] = new[p]
                return carry

            return lax.fori_loop(0, steps, one_step, carry)

        lax.fori_loop(0, BLKS, one_block, 0)


PLANE_SHAPE = (RELS, PLANES, TILES, 8, LANES)


def count_scratch(n):
    return [
        pltpu.VMEM((n, BLKS * TILES, 8, LANES), I32),
        pltpu.VMEM((2, 2, TILES, 8, LANES), I32),
        pltpu.SMEM((n, 8, LANES), I32),
        pltpu.SemaphoreType.DMA((n,)),
        pltpu.SemaphoreType.DMA((n,)),
    ]


def count_kernel(n, place_ref, *refs):
    edges = refs[:n]
    planes_ref, words, keys, meta, word_sems, meta_sems = refs[n + 1 :]
    loads = start_loads(edges, words, meta, word_sems, meta_sems)
    planes_ref[...] = refs[n][...]
    count_all(place_ref[0], loads, words, meta, keys, planes_ref)


def first_kernel(n, place_ref, *refs):
    edges = refs[:n]
    planes_ref, words, keys, meta, word_sems, meta_sems = refs[n:]
    loads = start_loads(edges, words, meta, word_sems, meta_sems)
    planes_ref[...] = jnp.zeros_like(planes_ref)
    count_all(place_ref[0], loads, words, meta, keys, planes_ref)


def count_first(place, edges):
    n = len(edges)
    return pl.pallas_call(
        functools.partial(first_kernel, n),
        out_shape=jax.ShapeDtypeStruct(PLANE_SHAPE, I32),
        in_specs=[pl.BlockSpec(memory_space=pltpu.SMEM)]
        + [pl.BlockSpec(memory_space=pl.ANY)] * n,
        out_specs=pl.BlockSpec(memory_space=pltpu.VMEM),
        scratch_shapes=count_scratch(n),
        compiler_params=pltpu.CompilerParams(vmem_limit_bytes=14 << 20),
        cost_estimate=pl.CostEstimate(
            flops=2_000_000_000, bytes_accessed=1 << 20, transcendentals=0
        ),
        name="count_first",
    )(place, *edges)


def count_edges(place, edges, planes):
    n = len(edges)
    vmem = pl.BlockSpec(memory_space=pltpu.VMEM)
    return pl.pallas_call(
        functools.partial(count_kernel, n),
        out_shape=jax.ShapeDtypeStruct(PLANE_SHAPE, I32),
        in_specs=[pl.BlockSpec(memory_space=pltpu.SMEM)]
        + [pl.BlockSpec(memory_space=pl.ANY)] * n
        + [vmem],
        out_specs=vmem,
        scratch_shapes=count_scratch(n),
        compiler_params=pltpu.CompilerParams(vmem_limit_bytes=14 << 20),
        cost_estimate=pl.CostEstimate(
            flops=n * 1_500_000_000, bytes_accessed=n << 19, transcendentals=0
        ),
        name="count_edges",
    )(place, *edges, planes)


def hidden_kernel(n, place_ref, *refs):
    edges, pieces = refs[:n], refs[n : n + 8]
    start_ref, out_ref, words, keys, meta, word_sems, meta_sems = refs[n + 8 : n + 15]
    planes_ref, adj, grads_vmem, sems = refs[n + 15 :]
    loads = start_loads(edges, words, meta, word_sems, meta_sems)
    copies = []
    for i in range(8):
        z = (place_ref[0] // 2 - i % 4) & 3
        core = place_ref[1] if i < 4 else 1 - place_ref[1]
        rows = pl.ds(pl.multiple_of((z * 2 + core) * PIECE, PIECE), PIECE)
        copies.append(pltpu.make_async_copy(pieces[i], grads_vmem.at[rows], sems.at[i]))
        copies[i].start()
    planes_ref[...] = start_ref[...]
    count_all(place_ref[0], loads, words, meta, keys, planes_ref)
    for r in range(RELS):
        for t in range(TILES):
            adj[r * OWN : (r + 1) * OWN, t * LANES : (t + 1) * LANES] = counts(
                [planes_ref[r, p, t] for p in range(PLANES)]
            )
    for copy in copies:
        copy.wait()
    wide = 2 * LANES
    for b in range(HID // wide):
        h = lax.dot_general(
            adj[...],
            grads_vmem[b * wide : (b + 1) * wide, :],
            (((1,), (1,)), ((), ())),
            preferred_element_type=F32,
        )
        h = (h * (1.0 / FANOUT)).astype(BF16)
        for r in range(RELS):
            to = r * HID + b * wide
            out_ref[:, to : to + wide] = h[r * OWN : (r + 1) * OWN, :]


def hidden_rows(place, edges, pieces, planes):
    n = len(edges)
    vmem = pl.BlockSpec(memory_space=pltpu.VMEM)
    return pl.pallas_call(
        functools.partial(hidden_kernel, n),
        out_shape=jax.ShapeDtypeStruct((OWN, COLS), BF16),
        in_specs=[pl.BlockSpec(memory_space=pltpu.SMEM)]
        + [pl.BlockSpec(memory_space=pl.ANY)] * (n + 8)
        + [vmem],
        out_specs=vmem,
        scratch_shapes=count_scratch(n)
        + [
            pltpu.VMEM(PLANE_SHAPE, I32),
            pltpu.VMEM((RELS * OWN, TGT), BF16),
            pltpu.VMEM((HID, TGT), BF16),
            pltpu.SemaphoreType.DMA((8,)),
        ],
        compiler_params=pltpu.CompilerParams(vmem_limit_bytes=20 << 20),
        cost_estimate=pl.CostEstimate(
            flops=6_000_000_000, bytes_accessed=4 << 20, transcendentals=0
        ),
        name="hidden_rows",
    )(place, *edges, *pieces, planes)


def after_kernel(*refs):
    pass


def after(values, earlier):
    n = len(values)
    anywhere = pl.BlockSpec(memory_space=pl.ANY)
    return pl.pallas_call(
        after_kernel,
        out_shape=[jax.ShapeDtypeStruct(v.shape, v.dtype) for v in values],
        in_specs=[anywhere] * (n + 1),
        out_specs=[anywhere] * n,
        input_output_aliases={i: i for i in range(n)},
        compiler_params=pltpu.CompilerParams(vmem_limit_bytes=1 << 20),
        cost_estimate=pl.CostEstimate(flops=1000, bytes_accessed=1 << 10, transcendentals=0),
        name="after",
    )(*values, earlier)


def source_kernel(hidden_ref, weight_ref, out_ref, done_ref):
    out_ref[...] = lax.dot_general(
        hidden_ref[...], weight_ref[...], (((1,), (1,)), ((), ())), preferred_element_type=F32
    ).astype(BF16)
    done_ref[...] = jnp.zeros_like(done_ref)


def source_rows(hidden, weight):
    vmem = pl.BlockSpec(memory_space=pltpu.VMEM)
    return pl.pallas_call(
        source_kernel,
        out_shape=[
            jax.ShapeDtypeStruct((OWN, D_IN), BF16),
            jax.ShapeDtypeStruct((8, LANES), F32),
        ],
        in_specs=[vmem] * 2,
        out_specs=[vmem] * 2,
        compiler_params=pltpu.CompilerParams(vmem_limit_bytes=16 << 20),
        cost_estimate=pl.CostEstimate(
            flops=20_000_000_000, bytes_accessed=6 << 20, transcendentals=0
        ),
        name="source_rows",
    )(hidden, weight)


def chunk_row(r, tile):
    return tile // 4 * 24 + tile // 2 % 2 * 12 + r * 2 + tile % 2


def product_kernel(h0_ref, h1_ref, f0_ref, f1_ref, earlier_ref, out_ref, chunks):
    wide = 2 * LANES
    for pair in range(COLS // (2 * wide)):
        parts = []
        for b in (2 * pair, 2 * pair + 1):
            cols = slice(b * wide, (b + 1) * wide)
            p = jnp.dot(f0_ref[...], h0_ref[:, cols], preferred_element_type=F32)
            p += jnp.dot(f1_ref[...], h1_ref[:, cols], preferred_element_type=F32)
            for r in range(ROWS_OUT):
                rows = p[r * PEERS : (r + 1) * PEERS]
                parts += [rows[:, c * LANES : (c + 1) * LANES] for c in range(2)]
        for g in range(3):
            at = pair * 24 + g * 8
            for d in range(0, PEERS, 8):
                block = jnp.stack([part[d : d + 8] for part in parts[g * 8 : (g + 1) * 8]], axis=0)
                chunks[d : d + 8, at : at + 8, :] = jnp.swapaxes(block, 0, 1)
    out_ref[...] = chunks[...].astype(BF16)


def products(h0, h1, f0, f1, earlier):
    vmem = pl.BlockSpec(memory_space=pltpu.VMEM)
    return pl.pallas_call(
        product_kernel,
        out_shape=jax.ShapeDtypeStruct((PEERS, CHUNK, LANES), BF16),
        in_specs=[vmem] * 4 + [pl.BlockSpec(memory_space=pl.ANY)],
        out_specs=vmem,
        scratch_shapes=[pltpu.VMEM((PEERS, CHUNK, LANES), F32)],
        compiler_params=pltpu.CompilerParams(vmem_limit_bytes=20 << 20),
        cost_estimate=pl.CostEstimate(
            flops=1_000_000_000, bytes_accessed=5 << 20, transcendentals=0
        ),
        name="products",
    )(h0, h1, f0, f1, earlier)


def sum_kernel(scale, got_ref, out_ref, sums):
    tiles = COLS // LANES
    total = got_ref[0].astype(F32)
    for d in range(1, PEERS):
        total += got_ref[d].astype(F32)
    sums[...] = total * scale
    for r in range(ROWS_OUT):
        for i in range(tiles):
            at = chunk_row(r, i)
            out_ref[r : r + 1, i * LANES : (i + 1) * LANES] = sums[at : at + 1, :]


def sum_chunks(got, scale):
    vmem = pl.BlockSpec(memory_space=pltpu.VMEM)
    return pl.pallas_call(
        functools.partial(sum_kernel, scale),
        out_shape=jax.ShapeDtypeStruct((ROWS_OUT, COLS), F32),
        in_specs=[vmem],
        out_specs=vmem,
        scratch_shapes=[pltpu.VMEM((CHUNK, LANES), F32)],
        compiler_params=pltpu.CompilerParams(vmem_limit_bytes=14 << 20),
        cost_estimate=pl.CostEstimate(flops=1 << 20, bytes_accessed=2 << 20, transcendentals=0),
        name="sum_chunks",
    )(got)


def on_device(grad_out, src_feat, weight, nbr_slot, src_ids, valid_rows, block_rel):
    rel = lax.axis_index("rel")
    core = rel & 1
    place = jnp.stack([rel, core]).astype(I32)

    def along_z(v, k):
        return lax.ppermute(v, "rel", [(i, (i + 2 * k) % 8) for i in range(8)])

    def other_core(v):
        return lax.ppermute(v, "rel", [(i, i ^ 1) for i in range(8)])

    codes = edge_codes(valid_rows, block_rel, src_ids[0], nbr_slot.transpose(1, 2, 0))
    far = {k: along_z(codes, k) for k in (1, 3)}
    own_grads = grad_out.T
    up, down = along_z(own_grads, 1), along_z(own_grads, 3)
    planes = count_first(place, [codes, other_core(codes)])
    far[1], down = after([far[1], down], planes)
    far[2], twice_down = along_z(far[1], 1), along_z(down, 3)
    planes = count_edges(place, [far[1], far[3]], planes)
    planes = count_edges(place, [other_core(far[1]), other_core(far[3])], planes)
    far[2], *pieces = after([far[2], up, twice_down, down], planes)
    pieces = [own_grads] + pieces
    pieces += [other_core(v) for v in pieces]

    old = jnp.arange(D_IN, dtype=I32)[:, None]
    new = jnp.arange(D_IN // 2, dtype=I32)[None, :]

    def half_feats(which):
        device = (new % PEERS) * 2 + which
        order = (old == device * ROWS_OUT + new // PEERS).astype(BF16)
        return lax.dot_general(
            order, src_feat, (((0,), (1,)), ((), ())), preferred_element_type=F32
        ).astype(BF16)

    feats = half_feats(core)
    feats_other = other_core(half_feats(1 - core))

    hidden = hidden_rows(place, [far[2], other_core(far[2])], pieces, planes)
    got = other_core(hidden)
    source_grad, done = source_rows(hidden, weight)
    chunks = products(hidden, got, feats, feats_other, done)
    groups = [[2 * i + c for i in range(PEERS)] for c in range(2)]
    chunks = lax.all_to_all(
        chunks, ("dp", "rel"), 0, 0, tiled=True, axis_index_groups=groups
    )
    return source_grad, sum_chunks(chunks, float(TGT * 16) ** (-0.5))


def solution(mesh):
    return jax.shard_map(
        on_device,
        mesh=mesh,
        in_specs=(
            P("dp", "rel"),
            P(("dp", "rel"), None),
            P(),
            P("dp", "rel", None),
            P("dp", "rel", None),
            P("dp", "rel"),
            P("rel"),
        ),
        out_specs=(P(("dp", "rel"), None), P(("dp", "rel"), None)),
        check_vma=False,
    )
```
